256 devices in a mesh: span: 16 (over y, x), chord: 8 (over z), wall: 2 (over core).
Axes of the slice: x: 4, y: 4, z: 8, core: 2. Of those that a mesh axis runs over, the one named last changes fastest.
Arguments:
- adjoint_start: float32 [5, 125, 32768], P(None, None, ('span', 'chord', 'wall')), may hold values from -6 to 6
- objective_grad: float32 [5, 125, 32768], P(None, None, ('span', 'chord', 'wall')), may hold values from -30 to 30
- conserved: float32 [5, 125, 32768], P(None, None, ('span', 'chord', 'wall'))
- metric_scale: float32 [32768], P(('span', 'chord', 'wall')), may hold values from 0.25 to 1
- time_step: float32 [32768], P(('span', 'chord', 'wall')), may hold values from 0.02 to 0.06
- viscosity: float32 [32768], P(('span', 'chord', 'wall')), may hold values from 0.05 to 0.4
- face_penalty: float32 [6, 32768], P(None, ('span', 'chord', 'wall')), may hold values from 2 to 8
- face_neighbor: int32 [6, 32768], P(None, ('span', 'chord', 'wall')), may hold values from -1 to 32767, as said below
- neighbor_face: int32 [6, 32768], P(None, ('span', 'chord', 'wall')), may hold values from 0 to 5
- face_orient: int32 [6, 32768], P(None, ('span', 'chord', 'wall')), may hold values from 0 to 3
- wall_elem: int32 [32768], P(('span', 'chord', 'wall')), may hold values from 0 to 127
- wall_face: int32 [32768], P(('span', 'chord', 'wall')), may hold values from 0 to 5
- wall_partial: float32 [3, 125, 32768], P(None, None, ('span', 'chord', 'wall')), may hold values from -0.5 to 0.5
- owner_device: int32 [32768, 1], P(('span', 'chord', 'wall')), may hold values from 0 to 255; in each aligned block of 128 rows (0 to 127, 128 to 255, ...) at most 2 rows name the same one
- owner_slot: int32 [32768], P(('span', 'chord', 'wall')), may hold values from 0 to 127
Outputs:
- adjoint: float32 [5, 125, 32768], P(None, None, ('span', 'chord', 'wall'))
- design_sens: float32 [3, 32768], P(None, ('span', 'chord', 'wall'))
The draws below stay inside these ranges and needn't reach their ends.
Inputs may be any that keep to these rules, and one draw needn't show every extreme that they name: `face_neighbor`: an element of partition p (p = element // 128, with partition p = (s * 8 + c) * 2 + w) has across each face either -1, an element of p, or an element of a partition whose (s, c, w) differs from p's by one in exactly one of the three. Over all faces of the elements of one partition, at most 64 name elements of one given other partition, and exactly 64 for every partition beside it. `owner_device`: among the wall faces of one partition, no owner partition is named more than 2 times, a bound that some block reaches.
All inputs are finite; a program needn't handle non-finite values.
Results may differ from the reference program's by a relative error of at most 0.0003.
Values sent between devices are 32-bit elements; how exact they have to be, the bound alone decides.
A program may use at most 320 MiB of HBM per device.

```python
import functools
import math
import jax
import jax.numpy as jnp
import numpy as np
from jax import lax

FIELDS = 5
NODES = 125
ITERS = 1
ELEM_DEV = 128
WALL_DEV = 128
DES_DEV = 128
SPAN_PARTS = 16
CHORD_PARTS = 8
WALL_PARTS = 2
PARTITIONS = 256
ELEMS = 32768
WALLS = 32768
DESIGN = 32768
CAP = 2
REQ = 64


def draw_conserved(key, part):
    subkeys = jax.random.split(key, 3)
    grid_shape = (125, ELEMS)
    density = jax.random.uniform(subkeys[0], grid_shape, jnp.float32, 0.8, 1.25)
    pressure = jax.random.uniform(subkeys[1], grid_shape, jnp.float32, 0.7, 1.4)
    velocity = 0.25 * jax.random.normal(subkeys[2], (3, 125, ELEMS), jnp.float32)
    velocity = velocity + jnp.array([0.6, 0.1, 0.0], jnp.float32)[:, None, None]
    energy = pressure / 0.4 + 0.5 * density * jnp.sum(velocity * velocity, axis=0)
    return jnp.concatenate([density[None], density[None] * velocity, energy[None]], axis=0)


def draw_face_neighbor(key, part):
    subkeys = jax.random.split(key, 4)
    grid_shape = (6, ELEMS)
    kind_draw = jax.random.randint(subkeys[0], grid_shape, 0, 10)
    local_index = jax.random.randint(subkeys[2], grid_shape, 0, ELEM_DEV)
    tie_break = jax.random.randint(subkeys[3], grid_shape, 0, 4096)
    elem_pos = (jnp.arange(ELEMS, dtype=jnp.int32) % ELEM_DEV)[None, :]
    order_key = (tie_break * ELEM_DEV + elem_pos).reshape(6, PARTITIONS, ELEM_DEV)
    ranking = jnp.argsort(jnp.argsort(order_key, axis=-1), axis=-1).reshape(6, ELEMS)
    eligible = ranking < REQ
    direction = jnp.arange(6, dtype=jnp.int32)[:, None]
    owner_part = (jnp.arange(ELEMS, dtype=jnp.int32) // ELEM_DEV)[None, :]
    span_pos = owner_part // (CHORD_PARTS * WALL_PARTS)
    chord_pos = owner_part // WALL_PARTS % CHORD_PARTS
    wall_pos = owner_part % WALL_PARTS
    step_sign = 2 * (direction % 2) - 1
    axis_pick = direction // 2
    new_span = span_pos + jnp.where(axis_pick == 0, step_sign, 0)
    new_chord = chord_pos + jnp.where(axis_pick == 1, step_sign, 0)
    new_wall = wall_pos + jnp.where(axis_pick == 2, step_sign, 0)
    inside = (new_span >= 0) & (new_span < SPAN_PARTS) & (new_chord >= 0) & (new_chord < CHORD_PARTS) & (new_wall >= 0) & (new_wall < WALL_PARTS)
    target = (new_span * CHORD_PARTS + new_chord) * WALL_PARTS + new_wall
    remote_link = target * ELEM_DEV + local_index
    local_link = owner_part * ELEM_DEV + local_index
    linked = jnp.where(eligible & inside, remote_link, jnp.where(kind_draw >= 8, -1, local_link))
    return linked.astype(jnp.int32)


def touch_ends(result, stream_key, least, top_value):
    index_at = [jax.random.randint(jax.random.fold_in(stream_key, axis), (), 0, length) for axis, length in enumerate(result.shape)]
    widest = result.shape.index(max(result.shape))
    neighbour = index_at[:widest] + [(index_at[widest] + 1) % result.shape[widest]] + index_at[widest + 1:]
    return result.at[tuple(index_at)].set(least).at[tuple(neighbour)].set(top_value)


def levels(stream_key, dims, shards, least, largest):
    gain, own = 1.0, jax.random.fold_in(stream_key, 6)
    for dim, blocks in shards:
        heights = jnp.exp(jax.random.uniform(jax.random.fold_in(own, dim), (blocks,), jnp.float32, least / len(shards), largest / len(shards)))
        gain = gain * jnp.repeat(heights, dims[dim] // blocks).reshape([-1 if axis == dim else 1 for axis in range(len(dims))])
    return gain


def shared_out(rng, own, number, rows, count, top, bound, skew):
    order = jax.random.permutation(rng, count)
    crowded, usual = shares(count, rows * top, bound, skew, True), shares(count, rows * top, bound, skew, False)
    places = jnp.arange(count)

    def named(lengths, turn):
        used = int((lengths > 0).sum())
        fixed = max(1, used // 4)
        shifted = fixed + (places - fixed + turn * (used - fixed)) % max(1, count - fixed)
        return jnp.zeros((count,), jnp.int32).at[order[jnp.where(places < fixed, places, shifted)]].set(jnp.asarray(lengths, jnp.int32))

    lengths = jnp.where(number % 4 == 0, named(crowded, number // 4), named(usual, number - number // 4 - 1))
    mixed = jax.random.permutation(jax.random.fold_in(own, 3), count)
    giver, taker = mixed[0:count // 2 * 2:2], mixed[1:count // 2 * 2:2]
    room = jnp.minimum(lengths[giver] - 1, bound - lengths[taker]) // 2
    room = jnp.where((giver == order[0]) | (taker == order[0]) | (lengths[taker] == 0), 0, jnp.maximum(room, 0))
    shifted = jax.random.randint(jax.random.fold_in(own, 4), (count // 2,), 0, 1 << 20) % (room + 1)
    lengths = lengths.at[giver].add(-shifted).at[taker].add(shifted)
    members = jnp.searchsorted(jnp.cumsum(lengths), jnp.arange(rows * top), side="right").astype(jnp.int32)
    listing = members.reshape(top, rows).T
    listing = listing[jax.random.permutation(jax.random.fold_in(own, 1), rows)]
    turn = jax.random.randint(jax.random.fold_in(own, 2), (rows, 1), 0, top)
    return jnp.take_along_axis(listing, (jnp.arange(top)[None, :] + turn) % top, axis=1)


def shares(number_of, total, reach, lean, full):
    loads = [(1 << 20) // math.isqrt(rank ** lean) + 1 for rank in range(1, number_of + 1)]
    largest = reach if full else min(reach, max(-(-total // number_of), total * loads[0] // sum(loads)))
    least = 1 if total - largest >= number_of - 1 else 0
    holding, spare = [largest] + [least] * (number_of - 1), total - largest - least * (number_of - 1)
    while spare > 0:
        free = [i for i in range(1, number_of) if holding[i] < largest] or [i for i in range(1, number_of) if holding[i] < reach]
        whole, budget = sum([loads[i] for i in free]), spare
        for i in free:
            extra = min(reach - holding[i], max(1, budget * loads[i] // whole), spare)
            holding[i] = holding[i] + extra
            spare = spare - extra
    return np.array(holding)


def noise(own_key, extent, spread, limit, cuts=(), kind=jnp.bfloat16):
    loudness = levels(own_key, extent, cuts, -0.22, 0.18) if cuts else 1.0
    entries = jax.random.normal(own_key, extent, jnp.float32) * spread * loudness
    return jnp.minimum(jnp.maximum(entries, -limit), limit).astype(kind)


def setup_inputs(seed: int = 0) -> dict:
    keys = jax.random.split(jax.random.key(seed), 16)
    adjoint_start = noise(keys[0], (FIELDS, NODES, ELEMS), 1.0, 6.0, ((2, 256),), jnp.float32)
    objective_grad = noise(keys[1], (FIELDS, NODES, ELEMS), 5.0, 30.0, ((2, 256),), jnp.float32)
    conserved = draw_conserved(jax.random.fold_in(keys[15], 71), 0)
    metric_scale = jnp.clip(jnp.exp(math.log(1.0) - 1.3862944 * jax.random.uniform(keys[3], (ELEMS,), jnp.float32) ** levels(keys[3], (ELEMS,), ((0, 256),), -0.2, 0.2)), 0.25, 1.0)
    time_step = jnp.clip(jnp.exp(math.log(0.06) - 1.0986123 * jax.random.uniform(keys[4], (ELEMS,), jnp.float32) ** levels(keys[4], (ELEMS,), ((0, 256),), -0.2, 0.2)), 0.02, 0.06)
    viscosity = jnp.clip(jnp.exp(math.log(0.4) - 2.0794415 * jax.random.uniform(keys[5], (ELEMS,), jnp.float32) ** levels(keys[5], (ELEMS,), ((0, 256),), -0.2, 0.2)), 0.05, 0.4)
    face_penalty = jnp.clip(jnp.exp(math.log(8.0) - 1.3862944 * jax.random.uniform(keys[6], (6, ELEMS), jnp.float32) ** levels(keys[6], (6, ELEMS), ((1, 256),), -0.2, 0.2)), 2.0, 8.0)
    face_neighbor = draw_face_neighbor(jax.random.fold_in(keys[15], 71), 0)
    neighbor_face = touch_ends(jax.random.randint(keys[8], (6, ELEMS), 0, 6), jax.random.fold_in(keys[8], 1), 0, 5).astype(jnp.int32)
    face_orient = touch_ends(jax.random.randint(keys[9], (6, ELEMS), 0, 4), jax.random.fold_in(keys[9], 1), 0, 3).astype(jnp.int32)
    wall_elem = touch_ends(jax.random.randint(keys[10], (WALLS,), 0, ELEM_DEV), jax.random.fold_in(keys[10], 1), 0, ELEM_DEV - 1).astype(jnp.int32)
    wall_face = touch_ends(jax.random.randint(keys[11], (WALLS,), 0, 6), jax.random.fold_in(keys[11], 1), 0, 5).astype(jnp.int32)
    wall_partial = noise(keys[12], (3, NODES, WALLS), NODES ** -0.5, 0.5, ((2, 256),), jnp.float32)
    owner_device_keys = jax.random.split(jax.random.fold_in(keys[13], 1), WALLS // WALL_DEV)
    owner_device_turns = jax.random.permutation(jax.random.fold_in(keys[13], 3), WALLS // WALL_DEV)
    owner_device = jax.vmap(lambda own, number: shared_out(jax.random.fold_in(keys[13], 2), own, number, WALL_DEV, PARTITIONS, 1, CAP, 1))(owner_device_keys, owner_device_turns).reshape((WALLS, 1))
    owner_slot = touch_ends(jax.random.randint(keys[14], (WALLS,), 0, DES_DEV), jax.random.fold_in(keys[14], 1), 0, DES_DEV - 1).astype(jnp.int32)
    return {"adjoint_start": adjoint_start, "objective_grad": objective_grad, "conserved": conserved, "metric_scale": metric_scale, "time_step": time_step, "viscosity": viscosity, "face_penalty": face_penalty, "face_neighbor": face_neighbor, "neighbor_face": neighbor_face, "face_orient": face_orient, "wall_elem": wall_elem, "wall_face": wall_face, "wall_partial": wall_partial, "owner_device": owner_device, "owner_slot": owner_slot}


GAMMA = 1.4

def derivative_table():
    points = [-1.0, -math.sqrt(3.0 / 7.0), 0.0, math.sqrt(3.0 / 7.0), 1.0]
    barycentric = []
    for i in range(5):
        product_value = 1.0
        for j in range(5):
            if j != i:
                product_value = product_value * (points[i] - points[j])
        barycentric.append(1.0 / product_value)
    matrix_values = np.zeros((5, 5))
    for i in range(5):
        for j in range(5):
            if j != i:
                matrix_values[i, j] = barycentric[j] / barycentric[i] / (points[i] - points[j])
        matrix_values[i, i] = -np.sum(matrix_values[i])
    return matrix_values

def sweep(field_five, axis_dir, transposed):
    matrix = jnp.asarray(derivative_table(), dtype=jnp.float32)
    contracted = 0 if transposed else 1
    contracted_field = jnp.tensordot(matrix, field_five, axes=((contracted,), (1 + axis_dir,)), precision=lax.Precision.HIGHEST)
    return jnp.moveaxis(contracted_field, 0, 1 + axis_dir)

def axis_flux(axis_dir, conserved):
    density = conserved[0]
    momentum = [conserved[1], conserved[2], conserved[3]]
    kinetic = 0.5 * (momentum[0] * momentum[0] + momentum[1] * momentum[1] + momentum[2] * momentum[2]) / density
    pressure = (GAMMA - 1.0) * (conserved[4] - kinetic)
    carried = momentum[axis_dir] / density
    columns = [momentum[axis_dir], momentum[0] * carried, momentum[1] * carried, momentum[2] * carried, (conserved[4] + pressure) * carried]
    columns[1 + axis_dir] = columns[1 + axis_dir] + pressure
    return jnp.stack(columns)

def volume_flux(conserved):
    return (axis_flux(0, conserved), axis_flux(1, conserved), axis_flux(2, conserved))

def face_trace(field_five, face):
    edge_index = 0 if face % 2 == 0 else 4
    return lax.index_in_dim(field_five, edge_index, 1 + face // 2, keepdims=False)

def add_to_face(field_five, face, face_term):
    edge_index = 0 if face % 2 == 0 else 4
    axis_dir = face // 2
    if axis_dir == 0:
        return field_five.at[:, edge_index].add(face_term)
    if axis_dir == 1:
        return field_five.at[:, :, edge_index].add(face_term)
    return field_five.at[:, :, :, edge_index].add(face_term)

def transposed_residual(adjoint, conserved, metric, viscosity, penalty, neighbor_trace):
    elements = adjoint.shape[-1]
    field_five = adjoint.reshape(5, 5, 5, 5, elements)
    state_five = conserved.reshape(5, 5, 5, 5, elements)
    weighted = tuple((sweep(field_five, axis_dir, True) for axis_dir in range(3)))
    primal_out, pullback = jax.vjp(volume_flux, state_five)
    volume = pullback(weighted)[0]
    viscous = sweep(weighted[0], 0, False) + sweep(weighted[1], 1, False) + sweep(weighted[2], 2, False)
    accumulated = metric * volume + viscosity * viscous
    for face in range(6):
        own_trace = face_trace(field_five, face)
        neighbor_part = neighbor_trace[:, :, :, face]
        face_state = face_trace(state_five, face)
        flux_out, face_pull = jax.vjp(functools.partial(axis_flux, face // 2), face_state)
        jacobian_term = face_pull(own_trace + neighbor_part)[0]
        normal_sign = 1.0 if face % 2 == 1 else -1.0
        face_term = penalty[face] * (own_trace - neighbor_part) + 0.5 * normal_sign * metric * jacobian_term
        accumulated = add_to_face(accumulated, face, face_term)
    return accumulated.reshape(5, 125, elements)

def pick_from_volume(gathered, neighbor_face):
    elements = gathered.shape[-1]
    field_six = gathered.reshape(5, 5, 5, 5, 6, elements)
    picked = jnp.zeros((5, 5, 5, 6, elements), gathered.dtype)
    for face in range(6):
        picked = jnp.where(neighbor_face == face, face_trace(field_six, face), picked)
    return picked

def orient_trace(picked, orientation, valid):
    oriented = jnp.where(orientation == 1, jnp.swapaxes(picked, 1, 2), picked)
    oriented = jnp.where(orientation == 2, jnp.flip(picked, 1), oriented)
    oriented = jnp.where(orientation == 3, jnp.flip(picked, 2), oriented)
    return jnp.where(valid, oriented, jnp.zeros_like(oriented))

def wall_sensitivity(adjoint, elem_index, face_index, partial_values):
    wall_count = elem_index.shape[0]
    volumes = jnp.take(adjoint, elem_index, axis=2).reshape(5, 5, 5, 5, wall_count)
    picked = jnp.zeros((5, 5, 5, wall_count), adjoint.dtype)
    for face in range(6):
        picked = jnp.where(face_index == face, face_trace(volumes, face), picked)
    return lax.optimization_barrier(jnp.sum(partial_values * picked.reshape(1, 125, wall_count), axis=1))

def reference(adjoint_start, objective_grad, conserved, metric_scale, time_step, viscosity, face_penalty, face_neighbor, neighbor_face, face_orient, wall_elem, wall_face, wall_partial, owner_device, owner_slot):

    def one_step(adjoint):

        def one_block(block_id):
            first_elem = (block_id * ELEM_DEV).astype(jnp.int32)

            def take_block(values):
                return lax.dynamic_slice_in_dim(values, first_elem, ELEM_DEV, values.ndim - 1)
            neighbor_ids = take_block(face_neighbor)
            gathered = jnp.take(adjoint, jnp.maximum(neighbor_ids, 0), axis=2)
            picked = pick_from_volume(gathered, take_block(neighbor_face))
            neighbor_trace = orient_trace(picked, take_block(face_orient), neighbor_ids >= 0)
            own_block = take_block(adjoint)
            residual = transposed_residual(own_block, take_block(conserved), take_block(metric_scale), take_block(viscosity), take_block(face_penalty), neighbor_trace)
            return own_block - take_block(time_step) * (residual - take_block(objective_grad))
        blocks = lax.map(one_block, jnp.arange(PARTITIONS, dtype=jnp.int32))
        return jnp.moveaxis(blocks, 0, 2).reshape(5, 125, ELEMS)
    adjoint = adjoint_start
    for round_number in range(ITERS):
        adjoint = one_step(adjoint)
    global_elem = jnp.arange(WALLS, dtype=jnp.int32) // WALL_DEV * ELEM_DEV + wall_elem
    values = wall_sensitivity(adjoint, global_elem, wall_face, wall_partial)
    design_ids = owner_device[:, 0] * DES_DEV + owner_slot
    design_sens = jax.ops.segment_sum(values.T, design_ids, num_segments=DESIGN).T
    return (adjoint, design_sens)
```

```python
import functools
import math

import jax
import jax.numpy as jnp
import numpy as np
from jax import lax
from jax.experimental import pallas as pl
from jax.experimental.pallas import tpu as pltpu
from jax.sharding import PartitionSpec as P

AXES = ("span", "chord", "wall")
MESH = pl.DeviceIdType.MESH
F32 = jnp.float32
BF16 = jnp.bfloat16
I32 = jnp.int32
E = 128
REQ = 64
HALO = 5
OPPOSITE = (1, 0, 3, 2, 4)
G = 0.4


def derivative_table():
    points = [-1.0, -math.sqrt(3.0 / 7.0), 0.0, math.sqrt(3.0 / 7.0), 1.0]
    barycentric = []
    for i in range(5):
        product_value = 1.0
        for j in range(5):
            if j != i:
                product_value = product_value * (points[i] - points[j])
        barycentric.append(1.0 / product_value)
    matrix_values = np.zeros((5, 5))
    for i in range(5):
        for j in range(5):
            if j != i:
                matrix_values[i, j] = barycentric[j] / barycentric[i] / (points[i] - points[j])
        matrix_values[i, i] = -np.sum(matrix_values[i])
    return matrix_values


def face_node(face, a, b):
    edge = 0 if face % 2 == 0 else 4
    index = {0: (edge, a, b), 1: (a, edge, b), 2: (a, b, edge)}[face // 2]
    return 25 * index[0] + 5 * index[1] + index[2]


def oriented(orient, a, b):
    return {0: (a, b), 1: (b, a), 2: (4 - a, b), 3: (a, 4 - b)}[orient]


def split_table(table):
    high = table.astype(np.float32).astype(jnp.bfloat16)
    low = (table - high.astype(np.float64)).astype(np.float32).astype(jnp.bfloat16)
    return high, low


@functools.cache
def tables():
    d = derivative_table()
    eye = np.eye(5)
    ends = np.zeros((5, 5))
    ends[0, 0], ends[4, 4] = -0.5, 0.5
    along = [
        lambda m: np.kron(m, np.kron(eye, eye)),
        lambda m: np.kron(eye, np.kron(m, eye)),
        lambda m: np.kron(eye, np.kron(eye, m)),
    ]
    sweeps = np.zeros((512, 128))
    for axis in range(3):
        sweeps[128 * axis : 128 * axis + 125, :125] = along[axis](d.T + ends)
        sweeps[384:509, :125] += along[axis](d) @ along[axis](d.T)
    sweep_high, sweep_low = split_table(sweeps)
    traces = np.zeros((192, 128))
    to_nodes = np.zeros((3, 128, 256))
    penalties = np.zeros((512, 32))
    for face in range(6):
        axis, sign = face // 2, (1.0 if face % 2 else -1.0)
        for a in range(5):
            for b in range(5):
                node = face_node(face, a, b)
                traces[32 * face + 5 * a + b, node] = 1.0
                for term in range(3):
                    penalties[128 * axis + node, 8 * term + face] = 2.0 * sign
                    penalties[384 + node, 8 * term + face] = 1.0
                for orient in range(4):
                    oa, ob = oriented(orient, a, b)
                    column = ((face % 2) * 4 + orient) * 32 + 5 * oa + ob
                    to_nodes[axis, node, column] = 0.5 * sign
    dense = np.zeros((128, 160))
    for field in range(5):
        for ab in range(25):
            dense[25 * field + ab, 32 * field + ab] = 1.0
    as_bf16 = lambda t: t.astype(np.float32).astype(jnp.bfloat16)
    return (
        np.concatenate([sweep_high, sweep_low], 0),
        as_bf16(traces),
        as_bf16(to_nodes),
        as_bf16(penalties),
        as_bf16(dense),
        as_bf16(dense.T.copy()),
    )


def split(x):
    high = x.astype(BF16)
    return high, (x - high.astype(F32)).astype(BF16)


def mm(a, b):
    return lax.dot_general(a, b, (((1,), (0,)), ((), ())), preferred_element_type=F32)


def mm_nt(a, b):
    return lax.dot_general(a, b, (((1,), (1,)), ((), ())), preferred_element_type=F32)


def iota(shape, dim):
    return lax.broadcasted_iota(I32, shape, dim)


def one_if(condition):
    return jnp.where(condition, 1.0, 0.0)


def kernel(
    sizes,
    psi_hbm,
    obj_hbm,
    u_hbm,
    wp_hbm,
    metric_hbm,
    dt_hbm,
    visc_hbm,
    pen_hbm,
    fn_hbm,
    nf_hbm,
    fo_hbm,
    we_hbm,
    wf_hbm,
    od_hbm,
    os_hbm,
    sweeps_hbm,
    traces_hbm,
    to_nodes_hbm,
    penalties_hbm,
    dense_hbm,
    dense_t_hbm,
    adj_hbm,
    sens_ref,
    metric_ref,
    dt_ref,
    visc_ref,
    pen_ref,
    fn_ref,
    nf_ref,
    fo_ref,
    we_ref,
    wf_ref,
    od_ref,
    os_ref,
    sweeps_ref,
    traces_ref,
    to_nodes_ref,
    penalties_ref,
    dense_ref,
    dense_t_ref,
    psi,
    obj,
    u,
    wp,
    wpad,
    adj,
    psib,
    xp,
    xd,
    local_hot,
    request_hot,
    req_out,
    req_in,
    resp_out,
    resp_in,
    swept,
    pen_nodes,
    rhs,
    jump,
    wall_hot,
    owner_hot,
    send_a,
    recv_a,
    send_b,
    recv_b,
    in_sem,
    out_sem,
    req_send_sem,
    req_recv_sem,
    resp_send_sem,
    resp_recv_sem,
    a_send_sem,
    a_recv_sem,
    b_send_sem,
    b_recv_sem,
):
    n_span, n_chord, n_wall = sizes
    n_plane = n_chord * n_wall
    s, c, w = (lax.axis_index(name) for name in AXES)
    part = (s * n_chord + c) * n_wall + w
    plane = c * n_wall + w

    sources = {
        "fn": (fn_hbm, fn_ref),
        "nf": (nf_hbm, nf_ref),
        "psi": (psi_hbm, psi),
        "traces": (traces_hbm, traces_ref),
        "dense": (dense_hbm, dense_ref),
        "sweeps": (sweeps_hbm, sweeps_ref),
        "pen": (pen_hbm, pen_ref),
        "penalties": (penalties_hbm, penalties_ref),
        "we": (we_hbm, we_ref),
        "wf": (wf_hbm, wf_ref),
        "wp": (wp_hbm, wp),
        "od": (od_hbm, od_ref),
        "os": (os_hbm, os_ref),
        "fo": (fo_hbm, fo_ref),
        "dense_t": (dense_t_hbm, dense_t_ref),
        "to_nodes": (to_nodes_hbm, to_nodes_ref),
        "u": (u_hbm, u),
        "obj": (obj_hbm, obj),
        "metric": (metric_hbm, metric_ref),
        "dt": (dt_hbm, dt_ref),
        "visc": (visc_hbm, visc_ref),
    }
    loads = {}
    for i, (name, (src, dst)) in enumerate(sources.items()):
        loads[name] = pltpu.make_async_copy(src, dst, in_sem.at[i])
        loads[name].start()

    def ready(*names):
        for name in names:
            loads[name].wait()

    barrier = pltpu.get_barrier_semaphore()
    for k in range(1, n_span):
        pl.semaphore_signal(
            barrier, inc=1, device_id=(lax.rem(s + k, n_span), c, w), device_id_type=MESH
        )
    for k in range(1, n_plane):
        there = lax.rem(plane + k, n_plane)
        pl.semaphore_signal(
            barrier,
            inc=1,
            device_id=(s, there // n_wall, lax.rem(there, n_wall)),
            device_id_type=MESH,
        )

    ready("fn", "nf")
    fn, nf = fn_ref[...], nf_ref[...]
    offset = jnp.where(fn >= 0, lax.shift_right_arithmetic(fn, 7) - part, 1 << 20)
    elem = jnp.bitwise_and(fn, E - 1)
    slot = iota((8, E), 0)
    wanted = jnp.where(slot == 4, 1 - 2 * w, 1 << 21)
    for j, step in enumerate((-n_plane, n_plane, -n_wall, n_wall)):
        wanted = jnp.where(slot == j, step, wanted)
    named = [offset[f : f + 1] == wanted for f in range(6)]
    before = jnp.concatenate(
        [one_if(iota((E, E), 0) < iota((E, E), 1)), jnp.ones((E, E), F32)], 1
    ).astype(BF16)
    counts = mm(jnp.concatenate([one_if(m) for m in named], 0).astype(BF16), before)
    base = jnp.zeros((8, E), F32)
    place = iota((REQ, E), 0).astype(F32)
    sub16 = iota((16, E), 0)
    codes = []
    for f in range(6):
        rank = jnp.where(named[f], counts[8 * f : 8 * f + 8, :E] + base, -1.0)
        base = base + counts[8 * f : 8 * f + 8, E:]
        for j in range(HALO):
            request_hot[REQ * j : REQ * (j + 1), E * f : E * (f + 1)] = one_if(
                rank[j : j + 1] == place
            ).astype(BF16)
        code = jnp.where(
            sub16 == 0, elem[f : f + 1], jnp.where(sub16 == 1, nf[f : f + 1], (sub16 == 2).astype(I32))
        )
        codes.append(code.astype(F32).astype(BF16))
    codes = jnp.concatenate(codes, 1)
    for j in range(HALO):
        got = mm_nt(codes, request_hot[REQ * j : REQ * (j + 1), :])
        req_out[j] = jnp.zeros((1, E), F32)
        req_out[j, :, 0:REQ] = got[0:1] + 128.0 * got[1:2] + 2048.0 * (1.0 - got[2:3])

    pl.semaphore_wait(barrier, n_span - 1 + n_plane - 1)
    beside = (
        (lax.rem(s + n_span - 1, n_span), c, w),
        (lax.rem(s + 1, n_span), c, w),
        (s, lax.rem(c + n_chord - 1, n_chord), w),
        (s, lax.rem(c + 1, n_chord), w),
        (s, c, 1 - w),
    )
    requests = [
        pltpu.make_async_remote_copy(
            src_ref=req_out.at[j],
            dst_ref=req_in.at[OPPOSITE[j]],
            send_sem=req_send_sem.at[j],
            recv_sem=req_recv_sem.at[OPPOSITE[j]],
            device_id=beside[j],
            device_id_type=MESH,
        )
        for j in range(HALO)
    ]
    for copy in requests:
        copy.start()

    ready("psi", "traces", "dense")
    for field in range(5):
        psib[0, 112:128, E * field : E * (field + 1)] = jnp.zeros((16, E), BF16)
        psib[1, 112:128, E * field : E * (field + 1)] = jnp.zeros((16, E), BF16)
        high, low = split(psi[field])
        psib[0, 0:125, E * field : E * (field + 1)] = high
        psib[1, 0:125, E * field : E * (field + 1)] = low
    for half in range(2):
        got = mm(traces_ref[...], psib[half]).astype(BF16)
        for field in range(5):
            for f in range(6):
                xp[160 * half + 32 * field : 160 * half + 32 * (field + 1), E * f : E * (f + 1)] = got[
                    32 * f : 32 * (f + 1), E * field : E * (field + 1)
                ]
        xd[128 * half : 128 * (half + 1), :] = mm(
            dense_ref[...], xp[160 * half : 160 * (half + 1), :]
        ).astype(BF16)

    for copy in requests:
        copy.wait_recv()
    asked = jnp.zeros((E, E), F32)
    rows = iota((E, E), 0)
    for j in range(HALO):
        asked = jnp.where(rows == j, req_in[j], asked)
    asked = asked.T
    columns = iota((REQ, 6 * E), 1).astype(F32)
    responses = []
    for j in range(HALO):
        hot = one_if(asked[0:REQ, j : j + 1] == columns).astype(BF16)
        got = mm_nt(hot, xd[...])
        resp_out[j] = got[:, :E] + got[:, E:]
        copy = pltpu.make_async_remote_copy(
            src_ref=resp_out.at[j],
            dst_ref=resp_in.at[OPPOSITE[j]],
            send_sem=resp_send_sem.at[j],
            recv_sem=resp_recv_sem.at[OPPOSITE[j]],
            device_id=beside[j],
            device_id_type=MESH,
        )
        copy.start()
        responses.append(copy)

    for f in range(6):
        code = jnp.where(offset[f : f + 1] == 0, elem[f : f + 1] + E * nf[f : f + 1], -1)
        for g in range(6):
            local_hot[E * g : E * (g + 1), E * f : E * (f + 1)] = one_if(
                code == iota((E, E), 0) + E * g
            ).astype(BF16)
    near = mm(xp[...], local_hot[...])
    ready("sweeps", "pen", "penalties")
    swept[...] = (
        mm(sweeps_ref[0:512], psib[0]) + mm(sweeps_ref[512:1024], psib[0]) + mm(sweeps_ref[0:512], psib[1])
    )
    pen8 = jnp.concatenate([pen_ref[...], jnp.zeros((2, E), F32)], 0)
    pen_high, pen_rest = pen8.astype(BF16), pen8
    pen_terms = []
    for _ in range(3):
        pen_high = pen_rest.astype(BF16).astype(F32)
        pen_terms.append(pen_high)
        pen_rest = pen_rest - pen_high
    pen_terms.append(jnp.zeros((8, E), F32))
    pen_nodes[...] = mm(penalties_ref[...], jnp.concatenate(pen_terms, 0).astype(BF16))

    ready("we", "wf", "wp", "od", "os", "fo", "dense_t", "to_nodes")
    fo = fo_ref[...]
    wall_code = we_ref[...] + E * wf_ref[...]
    for g in range(6):
        wall_hot[E * g : E * (g + 1), :] = one_if(wall_code == iota((E, E), 0) + E * g).astype(BF16)
    for x in range(3):
        for field in range(5):
            wpad[x, field] = jnp.zeros((32, E), F32)
            wpad[x, field, 0:25] = wp[x, 25 * field : 25 * (field + 1)]
    owner = od_ref[...]
    owner_rows = jnp.broadcast_to(owner.astype(F32), (E, E))
    owner_columns = owner_rows.T
    earlier = one_if((owner_rows == owner_columns) & (iota((E, E), 1) < iota((E, E), 0)))
    rank = jnp.sum(earlier, axis=1, keepdims=True)
    owner_span = lax.shift_right_arithmetic(owner, n_plane.bit_length() - 1)
    owner_plane = jnp.bitwise_and(owner_columns.astype(I32), n_plane - 1).astype(F32)
    lane = iota((E, E), 1).astype(F32)
    for v in range(4):
        owner_hot[E * v : E * (v + 1), :] = one_if(lane == 8.0 * owner_plane + rank + 2.0 * v).astype(BF16)
    to_span = one_if(iota((16, E), 0) == owner_span)

    for copy in responses:
        copy.wait_recv()
    answered = jnp.concatenate([resp_in[j] for j in range(HALO)], 0)
    answered_high, answered_low = split(answered)
    far = mm(
        jnp.concatenate(
            [mm_nt(dense_t_ref[...], answered_high), mm_nt(dense_t_ref[...], answered_low)], 0
        ).astype(BF16),
        request_hot[...],
    )
    found = near + far
    trace_high, trace_low = split(found[:160] + found[160:])
    for f in range(6):
        for o in range(4):
            mask = one_if(jnp.broadcast_to(fo[f : f + 1] == o, (32, E))).astype(BF16)
            row = ((f % 2) * 4 + o) * 32
            for field in range(5):
                for half, trace in enumerate((trace_high, trace_low)):
                    rhs[f // 2, 256 * half + row : 256 * half + row + 32, E * field : E * (field + 1)] = (
                        trace[32 * field : 32 * (field + 1), E * f : E * (f + 1)] * mask
                    )
    for axis in range(3):
        table = jnp.concatenate([to_nodes_ref[axis], to_nodes_ref[axis]], 1)
        jump[axis] = mm(table, rhs[axis])

    ready("u", "obj", "metric", "dt", "visc")
    metric, dt, visc = metric_ref[...], dt_ref[...], visc_ref[...]
    for field in range(5):
        adj[field, 120:128] = jnp.zeros((8, E), F32)
    for start in range(0, 125, 8):
        stop = min(start + 8, 125)
        cut = slice(start, stop)

        def lanes(field):
            return slice(E * field, E * (field + 1))

        rho, m1, m2, m3, energy = (u[field, cut] for field in range(5))
        inverse = 1.0 / rho
        vel = (m1 * inverse, m2 * inverse, m3 * inverse)
        kinetic = 0.5 * (vel[0] * vel[0] + vel[1] * vel[1] + vel[2] * vel[2])
        pressure = G * (energy - rho * kinetic)
        enthalpy = (energy + pressure) * inverse
        out = [0.0] * 5
        a_sum = 0.0
        diffused = []
        for axis in range(3):
            jumps = [jump[axis, cut, lanes(field)] for field in range(5)]
            wd = [
                swept[128 * axis + start : 128 * axis + stop, lanes(field)] + jumps[field]
                for field in range(5)
            ]
            pen = pen_nodes[128 * axis + start : 128 * axis + stop]
            diffused.append([pen * jumps[field] for field in range(5)])
            vd = vel[axis]
            carried = wd[1] * vel[0] + wd[2] * vel[1] + wd[3] * vel[2] + enthalpy * wd[4]
            a = wd[1 + axis] + vd * wd[4]
            a_sum = a_sum + a
            out[0] = out[0] - vd * carried
            for i in range(3):
                out[1 + i] = out[1 + i] + vd * wd[1 + i]
            out[1 + axis] = out[1 + axis] + (wd[0] + carried)
            out[4] = out[4] + vd * wd[4]
        ga = G * a_sum
        out[0] = out[0] + kinetic * ga
        for i in range(3):
            out[1 + i] = out[1 + i] - vel[i] * ga
        out[4] = out[4] + ga
        pen = pen_nodes[384 + start : 384 + stop]
        for field in range(5):
            old = psi[field, cut]
            residual = (
                metric * out[field]
                + visc * swept[384 + start : 384 + stop, lanes(field)]
                + (pen * old - (diffused[0][field] + diffused[1][field] + diffused[2][field]))
            )
            adj[field, cut] = old - dt * (residual - obj[field, cut])
    store = pltpu.make_async_copy(adj.at[:, 0:125], adj_hbm, out_sem)
    store.start()

    for field in range(5):
        high, low = split(adj[field])
        psib[0, :, E * field : E * (field + 1)] = high
        psib[1, :, E * field : E * (field + 1)] = low
    for half in range(2):
        got = mm(traces_ref[...], psib[half]).astype(BF16)
        for field in range(5):
            for f in range(6):
                xp[160 * half + 32 * field : 160 * half + 32 * (field + 1), E * f : E * (f + 1)] = got[
                    32 * f : 32 * (f + 1), E * field : E * (field + 1)
                ]
    taken = mm(xp[...], wall_hot[...])
    taken = taken[:160] + taken[160:]
    values = [os_ref[...].astype(F32)]
    for x in range(3):
        total = wpad[x, 0] * taken[0:32]
        for field in range(1, 5):
            total = total + wpad[x, field] * taken[32 * field : 32 * (field + 1)]
        values.append(jnp.sum(total, axis=0, keepdims=True))
    spread = jnp.concatenate([to_span * value for value in values], 1)
    terms = []
    for _ in range(3):
        term = spread.astype(BF16)
        terms.append(term)
        spread = spread - term.astype(F32)
    sent = mm(jnp.concatenate(terms, 0), owner_hot[...])
    sent = sent[0:16] + sent[16:32] + sent[32:48]

    for k in range(n_span):
        send_a[k] = sent[k : k + 1]
    copies = []
    for k in range(1, n_span):
        there = lax.rem(s + k, n_span)
        copy = pltpu.make_async_remote_copy(
            src_ref=send_a.at[there],
            dst_ref=recv_a.at[s],
            send_sem=a_send_sem.at[k],
            recv_sem=a_recv_sem.at[k],
            device_id=(there, c, w),
            device_id_type=MESH,
        )
        copy.start()
        copies.append(copy)
    recv_a[s] = send_a[s]
    for copy in copies:
        copy.wait_recv()
    arrived = jnp.zeros((E, E), F32)
    for k in range(n_span):
        arrived = jnp.where(rows == k, recv_a[k], arrived)
    arrived = arrived.T
    for k in range(n_plane):
        send_b[k] = arrived[8 * k : 8 * (k + 1)]
    copies_b = []
    for k in range(1, n_plane):
        there = lax.rem(plane + k, n_plane)
        copy = pltpu.make_async_remote_copy(
            src_ref=send_b.at[there],
            dst_ref=recv_b.at[plane],
            send_sem=b_send_sem.at[k],
            recv_sem=b_recv_sem.at[k],
            device_id=(s, there // n_wall, lax.rem(there, n_wall)),
            device_id_type=MESH,
        )
        copy.start()
        copies_b.append(copy)
    recv_b[plane] = send_b[plane]
    for copy in copies_b:
        copy.wait_recv()
    design = iota((8, E), 1).astype(F32)
    total = jnp.zeros((8, E), F32)
    for k in range(n_plane):
        block = recv_b[k]
        slots = jnp.concatenate([block[0:2]] * 4, 0)
        for j in range(n_span):
            total = total + jnp.where(slots[:, j : j + 1] == design, block[:, j : j + 1], 0.0)
    for x in range(3):
        sens_ref[x : x + 1] = total[2 + 2 * x : 3 + 2 * x] + total[3 + 2 * x : 4 + 2 * x]

    for copy in requests + responses + copies + copies_b:
        copy.wait_send()
    store.wait()


def on_device(sizes, *args):
    (psi, obj, u, metric, dt, visc, pen, fn, nf, fo, we, wf, wp, od, os_) = args
    row = lambda x: x.reshape(1, E)
    vmem = pl.BlockSpec(memory_space=pltpu.VMEM)
    hbm = pl.BlockSpec(memory_space=pltpu.HBM)
    n_span, n_chord, n_wall = sizes
    n_plane = n_chord * n_wall
    consts = tuple(jnp.asarray(t) for t in tables())
    return pl.pallas_call(
        functools.partial(kernel, sizes),
        out_shape=(
            jax.ShapeDtypeStruct((5, 125, E), F32),
            jax.ShapeDtypeStruct((3, E), F32),
        ),
        in_specs=[hbm] * (15 + len(consts)),
        out_specs=(hbm, vmem),
        scratch_shapes=[
            *[pltpu.VMEM((1, E), F32)] * 3,
            pltpu.VMEM((6, E), F32),
            *[pltpu.VMEM((6, E), I32)] * 3,
            *[pltpu.VMEM((1, E), I32)] * 4,
            *[pltpu.VMEM(t.shape, BF16) for t in consts],
            pltpu.VMEM((5, 125, E), F32),
            pltpu.VMEM((5, 125, E), F32),
            pltpu.VMEM((5, 125, E), F32),
            pltpu.VMEM((3, 125, E), F32),
            pltpu.VMEM((3, 5, 32, E), F32),
            pltpu.VMEM((5, 128, E), F32),
            pltpu.VMEM((2, 128, 5 * E), BF16),
            pltpu.VMEM((320, 6 * E), BF16),
            pltpu.VMEM((256, 6 * E), BF16),
            pltpu.VMEM((6 * E, 6 * E), BF16),
            pltpu.VMEM((HALO * REQ, 6 * E), BF16),
            pltpu.VMEM((HALO, 1, E), F32),
            pltpu.VMEM((HALO, 1, E), F32),
            pltpu.VMEM((HALO, REQ, E), F32),
            pltpu.VMEM((HALO, REQ, E), F32),
            pltpu.VMEM((512, 5 * E), F32),
            pltpu.VMEM((512, E), F32),
            pltpu.VMEM((3, 512, 5 * E), BF16),
            pltpu.VMEM((3, 128, 5 * E), F32),
            pltpu.VMEM((6 * E, E), BF16),
            pltpu.VMEM((4 * E, E), BF16),
            pltpu.VMEM((n_span, 1, E), F32),
            pltpu.VMEM((n_span, 1, E), F32),
            pltpu.VMEM((n_plane, 8, E), F32),
            pltpu.VMEM((n_plane, 8, E), F32),
            pltpu.SemaphoreType.DMA((15 + len(consts),)),
            pltpu.SemaphoreType.DMA,
            pltpu.SemaphoreType.DMA((HALO,)),
            pltpu.SemaphoreType.DMA((HALO,)),
            pltpu.SemaphoreType.DMA((HALO,)),
            pltpu.SemaphoreType.DMA((HALO,)),
            pltpu.SemaphoreType.DMA((n_span,)),
            pltpu.SemaphoreType.DMA((n_span,)),
            pltpu.SemaphoreType.DMA((n_plane,)),
            pltpu.SemaphoreType.DMA((n_plane,)),
        ],
        compiler_params=pltpu.CompilerParams(
            collective_id=0, has_side_effects=True, vmem_limit_bytes=60 * 2**20
        ),
        name="adjoint_step",
    )(
        psi,
        obj,
        u,
        wp,
        row(metric),
        row(dt),
        row(visc),
        pen,
        fn,
        nf,
        fo,
        row(we),
        row(wf),
        row(od),
        row(os_),
        *consts,
    )


def solution(mesh):
    whole = P(None, None, AXES)
    plane = P(None, AXES)
    line = P(AXES)
    in_specs = (
        (whole,) * 3 + (line,) * 3 + (plane,) * 4 + (line,) * 2 + (whole, P(AXES, None), line)
    )
    sizes = tuple(mesh.shape[name] for name in AXES)
    return jax.shard_map(
        functools.partial(on_device, sizes),
        mesh=mesh,
        in_specs=in_specs,
        out_specs=(whole, plane),
        check_vma=False,
    )
```

```python
import functools
import math

import jax
import jax.numpy as jnp
import numpy as np
from jax import lax
from jax.experimental import pallas as pl
from jax.experimental.pallas import tpu as pltpu
from jax.sharding import PartitionSpec as P

AXES = ("span", "chord", "wall")
MESH = pl.DeviceIdType.MESH
F32 = jnp.float32
BF16 = jnp.bfloat16
I32 = jnp.int32
E = 128
REQ = 64
HALO = 5
OPPOSITE = (1, 0, 3, 2, 4)
G = 0.4


def derivative_table():
    points = [-1.0, -math.sqrt(3.0 / 7.0), 0.0, math.sqrt(3.0 / 7.0), 1.0]
    barycentric = []
    for i in range(5):
        product_value = 1.0
        for j in range(5):
            if j != i:
                product_value = product_value * (points[i] - points[j])
        barycentric.append(1.0 / product_value)
    matrix_values = np.zeros((5, 5))
    for i in range(5):
        for j in range(5):
            if j != i:
                matrix_values[i, j] = barycentric[j] / barycentric[i] / (points[i] - points[j])
        matrix_values[i, i] = -np.sum(matrix_values[i])
    return matrix_values


def face_node(face, a, b):
    edge = 0 if face % 2 == 0 else 4
    index = {0: (edge, a, b), 1: (a, edge, b), 2: (a, b, edge)}[face // 2]
    return 25 * index[0] + 5 * index[1] + index[2]


def oriented(orient, a, b):
    return {0: (a, b), 1: (b, a), 2: (4 - a, b), 3: (a, 4 - b)}[orient]


def split_table(table):
    high = table.astype(np.float32).astype(jnp.bfloat16)
    low = (table - high.astype(np.float64)).astype(np.float32).astype(jnp.bfloat16)
    return high, low


@functools.cache
def tables():
    d = derivative_table()
    eye = np.eye(5)
    ends = np.zeros((5, 5))
    ends[0, 0], ends[4, 4] = -0.5, 0.5
    along = [
        lambda m: np.kron(m, np.kron(eye, eye)),
        lambda m: np.kron(eye, np.kron(m, eye)),
        lambda m: np.kron(eye, np.kron(eye, m)),
    ]
    sweeps = np.zeros((512, 128))
    for axis in range(3):
        sweeps[128 * axis : 128 * axis + 125, :125] = along[axis](d.T + ends)
        sweeps[384:509, :125] += along[axis](d) @ along[axis](d.T)
    sweep_high, sweep_low = split_table(sweeps)
    traces = np.zeros((192, 128))
    to_nodes = np.zeros((3, 128, 128))
    turns = np.zeros((160, 512))
    penalties = np.zeros((512, 32))
    for face in range(6):
        axis, sign = face // 2, (1.0 if face % 2 else -1.0)
        for a in range(5):
            for b in range(5):
                node = face_node(face, a, b)
                traces[32 * face + 5 * a + b, node] = 1.0
                for term in range(3):
                    penalties[128 * axis + node, 8 * term + face] = 2.0 * sign
                    penalties[384 + node, 8 * term + face] = 1.0
                for term in range(2):
                    to_nodes[axis, node, 64 * term + 32 * (face % 2) + 5 * a + b] = 0.5 * sign
    dense = np.zeros((128, 160))
    for field in range(5):
        for ab in range(25):
            dense[25 * field + ab, 32 * field + ab] = 1.0
            for orient in range(4):
                oa, ob = oriented(orient, ab // 5, ab % 5)
                turns[32 * field + ab, 128 * orient + 25 * field + 5 * oa + ob] = 1.0
    as_bf16 = lambda t: t.astype(np.float32).astype(jnp.bfloat16)
    return (
        np.concatenate([sweep_high, sweep_low], 0),
        as_bf16(traces),
        as_bf16(to_nodes),
        as_bf16(penalties),
        as_bf16(dense),
        as_bf16(turns),
    )


def split(x):
    high = x.astype(BF16)
    return high, (x - high.astype(F32)).astype(BF16)


def mm(a, b):
    return lax.dot_general(a, b, (((1,), (0,)), ((), ())), preferred_element_type=F32)


def mm_nt(a, b):
    return lax.dot_general(a, b, (((1,), (1,)), ((), ())), preferred_element_type=F32)


def iota(shape, dim):
    return lax.broadcasted_iota(I32, shape, dim)


def one_if(condition):
    return jnp.where(condition, 1.0, 0.0)


def far_first(n):
    return sorted(range(1, n), key=lambda k: -min(k, n - k))


def whole(ref, sem):
    return pltpu.make_async_copy(ref, ref, sem)


def kernel(
    sizes,
    psi_hbm,
    obj_hbm,
    u_hbm,
    wp_hbm,
    metric_hbm,
    dt_hbm,
    visc_hbm,
    pen_hbm,
    fn_hbm,
    nf_hbm,
    fo_hbm,
    we_hbm,
    wf_hbm,
    od_hbm,
    os_hbm,
    sweeps_hbm,
    traces_hbm,
    to_nodes_hbm,
    penalties_hbm,
    dense_hbm,
    turns_hbm,
    adj_out,
    entries_ref,
    metric_ref,
    dt_ref,
    visc_ref,
    pen_ref,
    fn_ref,
    nf_ref,
    fo_ref,
    we_ref,
    wf_ref,
    od_ref,
    os_ref,
    sweeps_ref,
    traces_ref,
    to_nodes_ref,
    penalties_ref,
    dense_ref,
    turns_ref,
    psi,
    obj,
    u,
    wp,
    wpad,
    adj,
    psib,
    xp,
    xd,
    local_hot,
    request_hot,
    req_out,
    req_in,
    resp_out,
    resp_in,
    swept,
    pen_nodes,
    local_turned,
    near,
    far_masks,
    state,
    jump,
    wall_hot,
    owner_hot,
    send_a,
    recv_a,
    send_b,
    recv_b,
    in_sem,
    req_send_sem,
    req_recv_sem,
    resp_send_sem,
    resp_recv_sem,
    a_send_sem,
    a_recv_sem,
    b_send_sem,
    b_recv_sem,
    round2_sem,
    round3_sem,
    round4_sem,
):
    n_span, n_chord, n_wall = sizes
    n_plane = n_chord * n_wall
    s, c, w = (lax.axis_index(name) for name in AXES)
    part = (s * n_chord + c) * n_wall + w
    plane = c * n_wall + w

    def in_plane(k):
        there = jnp.bitwise_and(plane + k, n_plane - 1)
        return (s, lax.shift_right_arithmetic(there, n_wall.bit_length() - 1), jnp.bitwise_and(there, n_wall - 1))


    sources = {
        "fn": (fn_hbm, fn_ref),
        "nf": (nf_hbm, nf_ref),
        "psi": (psi_hbm, psi),
        "traces": (traces_hbm, traces_ref),
        "dense": (dense_hbm, dense_ref),
        "sweeps": (sweeps_hbm, sweeps_ref),
        "fo": (fo_hbm, fo_ref),
        "pen": (pen_hbm, pen_ref),
        "dt": (dt_hbm, dt_ref),
        "penalties": (penalties_hbm, penalties_ref),
        "we": (we_hbm, we_ref),
        "wf": (wf_hbm, wf_ref),
        "wp": (wp_hbm, wp),
        "od": (od_hbm, od_ref),
        "os": (os_hbm, os_ref),
        "turns": (turns_hbm, turns_ref),
        "to_nodes": (to_nodes_hbm, to_nodes_ref),
        "u": (u_hbm, u),
        "obj": (obj_hbm, obj),
        "metric": (metric_hbm, metric_ref),
        "visc": (visc_hbm, visc_ref),
    }
    loads = {}
    for i, (name, (src, dst)) in enumerate(sources.items()):
        loads[name] = pltpu.make_async_copy(src, dst, in_sem.at[i])
        loads[name].start()

    def ready(*names):
        for name in names:
            loads[name].wait()

    barrier = pltpu.get_barrier_semaphore()
    def along(ds, dc, other=False):
        return (
            jnp.bitwise_and(s + ds, n_span - 1),
            jnp.bitwise_and(c + dc, n_chord - 1),
            1 - w if other else w,
        )

    def greet(sem, near_chord):
        for peer in (
            along(1, 0),
            along(-1, 0),
            along(4, 0),
            along(-4, 0),
            along(0, near_chord),
            along(0, -near_chord),
            along(0, 0, True),
        ):
            pl.semaphore_signal(sem, inc=1, device_id=peer, device_id_type=MESH)

    greet(barrier, 1)

    ready("fn", "nf")
    fn, nf = fn_ref[...], nf_ref[...]
    offset = jnp.where(fn >= 0, lax.shift_right_arithmetic(fn, 7) - part, 1 << 20)
    elem = jnp.bitwise_and(fn, E - 1)
    slot = iota((8, E), 0)
    wanted = jnp.where(slot == 4, 1 - 2 * w, 1 << 21)
    for j, step in enumerate((-n_plane, n_plane, -n_wall, n_wall)):
        wanted = jnp.where(slot == j, step, wanted)
    named = [offset[f : f + 1] == wanted for f in range(6)]
    before = jnp.concatenate(
        [one_if(iota((E, E), 0) < iota((E, E), 1)), jnp.ones((E, E), F32)], 1
    ).astype(BF16)
    counts = mm(jnp.concatenate([one_if(m) for m in named], 0).astype(BF16), before)
    base = jnp.zeros((8, E), F32)
    place = iota((REQ, E), 0).astype(F32)
    sub16 = iota((16, E), 0)
    codes = []
    for f in range(6):
        rank = jnp.where(named[f], counts[8 * f : 8 * f + 8, :E] + base, -1.0)
        base = base + counts[8 * f : 8 * f + 8, E:]
        for j in range(HALO):
            request_hot[REQ * j : REQ * (j + 1), E * f : E * (f + 1)] = one_if(
                rank[j : j + 1] == place
            ).astype(BF16)
        code = jnp.where(
            sub16 == 0, elem[f : f + 1], jnp.where(sub16 == 1, nf[f : f + 1], (sub16 == 2).astype(I32))
        )
        codes.append(code.astype(F32).astype(BF16))
    codes = jnp.concatenate(codes, 1)
    for j in range(HALO):
        got = mm_nt(codes, request_hot[REQ * j : REQ * (j + 1), :])
        req_out[j] = jnp.zeros((1, E), F32)
        req_out[j, :, 0:REQ] = got[0:1] + 128.0 * got[1:2] + 2048.0 * (1.0 - got[2:3])

    pl.semaphore_wait(barrier, 7)
    beside = (along(-1, 0), along(1, 0), along(0, -1), along(0, 1), along(0, 0, True))
    requests = [
        pltpu.make_async_remote_copy(
            src_ref=req_out.at[j],
            dst_ref=req_in.at[OPPOSITE[j]],
            send_sem=req_send_sem,
            recv_sem=req_recv_sem,
            device_id=beside[j],
            device_id_type=MESH,
        )
        for j in range(HALO)
    ]
    for copy in requests:
        copy.start()
    greet(round2_sem, 1)

    ready("psi", "traces", "dense")
    for field in range(5):
        psib[0, 112:128, E * field : E * (field + 1)] = jnp.zeros((16, E), BF16)
        psib[1, 112:128, E * field : E * (field + 1)] = jnp.zeros((16, E), BF16)
        high, low = split(psi[field])
        psib[0, 0:125, E * field : E * (field + 1)] = high
        psib[1, 0:125, E * field : E * (field + 1)] = low
    for half in range(2):
        got = mm(traces_ref[...], psib[half]).astype(BF16)
        for field in range(5):
            for f in range(6):
                xp[160 * half + 32 * field : 160 * half + 32 * (field + 1), E * f : E * (f + 1)] = got[
                    32 * f : 32 * (f + 1), E * field : E * (field + 1)
                ]
        xd[128 * half : 128 * (half + 1), :] = mm(
            dense_ref[...], xp[160 * half : 160 * (half + 1), :]
        ).astype(BF16)

    slots8 = iota((8, E), 0)
    mine = jnp.full((8, E), -1, I32)
    for f in range(6):
        code = jnp.where(offset[f : f + 1] == 0, elem[f : f + 1] + E * nf[f : f + 1], -1)
        mine = jnp.where(slots8 == f, code, mine)
    ready("fo")
    fo = fo_ref[...]
    turned = jnp.concatenate(
        [mine.astype(F32), fo.astype(F32), jnp.zeros((E - 14, E), F32)], 0
    ).T
    columns = iota((E, 6 * E), 1).astype(F32)
    for f in range(6):
        local_hot[E * f : E * (f + 1), :] = one_if(turned[:, f : f + 1] == columns).astype(BF16)
    ready("sweeps", "pen", "penalties", "dt")
    swept[...] = (
        mm(sweeps_ref[0:512], psib[0]) + mm(sweeps_ref[512:1024], psib[0]) + mm(sweeps_ref[0:512], psib[1])
    )
    pen8 = jnp.concatenate([pen_ref[...], jnp.zeros((2, E), F32)], 0)
    pen_terms = []
    for _ in range(3):
        pen_high = pen8.astype(BF16).astype(F32)
        pen_terms.append(pen_high)
        pen8 = pen8 - pen_high
    pen_terms.append(jnp.zeros((8, E), F32))
    pen_nodes[...] = dt_ref[...] * mm(penalties_ref[...], jnp.concatenate(pen_terms, 0).astype(BF16))

    own_answers = mm_nt(local_hot[...], xd[...]).astype(BF16)
    for f in range(6):
        seen = jnp.broadcast_to(turned[:, 8 + f : 9 + f], (E, E))
        for o in range(4):
            mask = one_if(seen == o).astype(BF16)
            for half in range(2):
                local_turned[E * f : E * (f + 1), 512 * half + E * o : 512 * half + E * (o + 1)] = (
                    own_answers[E * f : E * (f + 1), E * half : E * (half + 1)] * mask
                )
    ready("turns")
    turns2 = jnp.concatenate([turns_ref[...], turns_ref[...]], 1)
    near[...] = mm_nt(turns2, local_turned[...])
    whole(req_in, req_recv_sem).wait()
    pl.semaphore_wait(round2_sem, 7)
    asked = jnp.zeros((8, E), F32)
    for j in range(HALO):
        asked = jnp.where(slots8 == j, req_in[j], asked)
    asked = jnp.concatenate([asked, jnp.zeros((E - 8, E), F32)], 0).T
    columns = iota((REQ, 6 * E), 1).astype(F32)
    for j in range(HALO):
        hot = one_if(asked[0:REQ, j : j + 1] == columns).astype(BF16)
        got = mm_nt(hot, xd[...])
        resp_out[j] = got[:, :E] + got[:, E:]
        copy = pltpu.make_async_remote_copy(
            src_ref=resp_out.at[j],
            dst_ref=resp_in.at[OPPOSITE[j]],
            send_sem=resp_send_sem,
            recv_sem=resp_recv_sem,
            device_id=beside[j],
            device_id_type=MESH,
        )
        copy.start()

    greet(round3_sem, 2)
    views = jnp.concatenate(
        [jnp.broadcast_to(fo[f : f + 1], (16, E)).astype(F32).astype(BF16) for f in range(6)], 1
    )
    views = mm_nt(request_hot[...], jnp.concatenate([views] * 8, 0))
    for o in range(4):
        far_masks[o] = one_if(views == o).astype(BF16)

    ready("we", "wf", "wp", "od", "os")
    wall_code = we_ref[...] + E * wf_ref[...]
    for g in range(6):
        wall_hot[E * g : E * (g + 1), :] = one_if(wall_code == iota((E, E), 0) + E * g).astype(BF16)
    for x in range(3):
        for field in range(5):
            wpad[x, field] = jnp.zeros((32, E), F32)
            wpad[x, field, 0:25] = wp[x, 25 * field : 25 * (field + 1)]
    owner = od_ref[...]
    owner_rows = jnp.broadcast_to(owner.astype(F32), (E, E))
    owner_columns = owner_rows.T
    earlier = one_if((owner_rows == owner_columns) & (iota((E, E), 1) < iota((E, E), 0)))
    rank = jnp.sum(earlier, axis=1, keepdims=True)
    owner_span = lax.shift_right_arithmetic(owner, n_plane.bit_length() - 1)
    owner_plane = jnp.bitwise_and(owner_columns.astype(I32), n_plane - 1).astype(F32)
    lane = iota((E, E), 1).astype(F32)
    for v in range(4):
        owner_hot[E * v : E * (v + 1), :] = one_if(lane == owner_plane + 16.0 * rank + 32.0 * v).astype(BF16)
    to_span = one_if(iota((16, E), 0) == owner_span)

    ready("u", "obj", "metric", "visc")
    metric, dt, visc = metric_ref[...], dt_ref[...], visc_ref[...]
    dt_metric, dt_visc = dt * metric, dt * visc

    def lanes(field):
        return slice(E * field, E * (field + 1))

    def transposed_flux(axes, vel, kinetic, enthalpy, weights):
        out = [0.0] * 5
        a_sum = 0.0
        for axis in axes:
            wd, vd = weights[axis], vel[axis]
            carried = wd[1] * vel[0] + wd[2] * vel[1] + wd[3] * vel[2] + enthalpy * wd[4]
            a_sum = a_sum + (wd[1 + axis] + vd * wd[4])
            out[0] = out[0] - vd * carried
            for i in range(3):
                out[1 + i] = out[1 + i] + vd * wd[1 + i]
            out[1 + axis] = out[1 + axis] + (wd[0] + carried)
            out[4] = out[4] + vd * wd[4]
        ga = G * a_sum
        out[0] = out[0] + kinetic * ga
        for i in range(3):
            out[1 + i] = out[1 + i] - vel[i] * ga
        out[4] = out[4] + ga
        return out

    for start in range(0, 125, 8):
        stop = min(start + 8, 125)
        cut = slice(start, stop)
        rho, m1, m2, m3, energy = (u[field, cut] for field in range(5))
        inverse = 1.0 / rho
        vel = (m1 * inverse, m2 * inverse, m3 * inverse)
        kinetic = 0.5 * (vel[0] * vel[0] + vel[1] * vel[1] + vel[2] * vel[2])
        pressure = G * (energy - rho * kinetic)
        enthalpy = (energy + pressure) * inverse
        for i, kept in enumerate((*vel, kinetic, enthalpy)):
            state[i, cut] = kept
        weights = [
            [swept[128 * axis + start : 128 * axis + stop, lanes(field)] for field in range(5)]
            for axis in range(3)
        ]
        out = transposed_flux(range(3), vel, kinetic, enthalpy, weights)
        pen = 1.0 - pen_nodes[384 + start : 384 + stop]
        for field in range(5):
            adj[field, cut] = (
                pen * psi[field, cut]
                + dt * obj[field, cut]
                - dt_metric * out[field]
                - dt_visc * swept[384 + start : 384 + stop, lanes(field)]
            )
    for field in range(5):
        adj[field, 125:128] = jnp.zeros((3, E), F32)
    ready("to_nodes")

    whole(resp_in, resp_recv_sem).wait()
    pl.semaphore_wait(round3_sem, 7)
    pl.semaphore_signal(round4_sem, inc=1, device_id=along(0, 0, True), device_id_type=MESH)
    answered = jnp.concatenate([resp_in[j] for j in range(HALO)], 0)
    answered = split(answered)
    placed = []
    for half in range(2):
        masked = jnp.concatenate([answered[half] * far_masks[o] for o in range(4)], 1)
        placed.append(mm_nt(turns_ref[...], masked).astype(BF16))
    far = mm(jnp.concatenate(placed, 0), request_hot[...])
    trace = split(near[...] + (far[:160] + far[160:]))
    for axis in range(3):
        rhs = jnp.concatenate(
            [
                jnp.concatenate(
                    [
                        trace[half][32 * field : 32 * (field + 1), E * f : E * (f + 1)]
                        for half in range(2)
                        for f in (2 * axis, 2 * axis + 1)
                    ],
                    0,
                )
                for field in range(5)
            ],
            1,
        )
        jump[axis] = mm(to_nodes_ref[axis], rhs)

    for start in range(0, 125, 8):
        stop = min(start + 8, 125)
        cut = slice(start, stop)
        axes = range(3) if start < 25 or stop > 100 else range(1, 3)
        vel = tuple(state[i, cut] for i in range(3))
        weights = [[jump[axis, cut, lanes(field)] for field in range(5)] for axis in range(3)]
        out = transposed_flux(axes, vel, state[3, cut], state[4, cut], weights)
        for field in range(5):
            new = adj[field, cut] - dt_metric * out[field]
            for axis in axes:
                new = new + pen_nodes[128 * axis + start : 128 * axis + stop] * weights[axis][field]
            adj[field, cut] = new
            adj_out[field, cut] = new

    for field in range(5):
        high, low = split(adj[field])
        psib[0, :, E * field : E * (field + 1)] = high
        psib[1, :, E * field : E * (field + 1)] = low
    for half in range(2):
        got = mm(traces_ref[...], psib[half]).astype(BF16)
        for field in range(5):
            for f in range(6):
                xp[160 * half + 32 * field : 160 * half + 32 * (field + 1), E * f : E * (f + 1)] = got[
                    32 * f : 32 * (f + 1), E * field : E * (field + 1)
                ]
    taken = mm(xp[...], wall_hot[...])
    taken = taken[:160] + taken[160:]
    values = [os_ref[...].astype(F32)]
    for x in range(3):
        total = wpad[x, 0] * taken[0:32]
        for field in range(1, 5):
            total = total + wpad[x, field] * taken[32 * field : 32 * (field + 1)]
        values.append(jnp.sum(total, axis=0, keepdims=True))
    spread = jnp.concatenate([to_span * value for value in values], 1)
    terms = []
    for _ in range(3):
        term = spread.astype(BF16)
        terms.append(term)
        spread = spread - term.astype(F32)
    sent = mm(jnp.concatenate(terms, 0), owner_hot[...])
    sent = sent[0:16] + sent[16:32] + sent[32:48]

    for k in range(n_span):
        send_a[k] = sent[k : k + 1]
    for k in far_first(n_span):
        there = jnp.bitwise_and(s + k, n_span - 1)
        pltpu.make_async_remote_copy(
            src_ref=send_a.at[there],
            dst_ref=recv_a.at[k],
            send_sem=a_send_sem,
            recv_sem=a_recv_sem,
            device_id=(there, c, w),
            device_id_type=MESH,
        ).start()
    recv_a[0] = send_a[s]
    whole(recv_a.at[1:n_span], a_recv_sem).wait()
    sub16 = iota((16, E), 0)
    arrived = jnp.zeros((16, E), F32)
    for k in range(n_span):
        arrived = jnp.where(sub16 == k, recv_a[k], arrived)
    arrived = jnp.concatenate([arrived, jnp.zeros((E - 16, E), F32)], 0).T
    onward = arrived[0:16]
    for i in range(1, 8):
        onward = onward + pltpu.roll(arrived[16 * i : 16 * (i + 1)], 16 * i, 1)
    for k in range(n_plane):
        send_b[k] = onward[k : k + 1]
    pl.semaphore_wait(round4_sem, 1)
    for k in far_first(n_plane):
        there = jnp.bitwise_and(plane + k, n_plane - 1)
        pltpu.make_async_remote_copy(
            src_ref=send_b.at[there],
            dst_ref=recv_b.at[k],
            send_sem=b_send_sem,
            recv_sem=b_recv_sem,
            device_id=in_plane(k),
            device_id_type=MESH,
        ).start()
    recv_b[0] = send_b[plane]
    whole(req_out, req_send_sem).wait()
    whole(resp_out, resp_send_sem).wait()
    whole(send_a.at[1:n_span], a_send_sem).wait()
    whole(recv_b.at[1:n_plane], b_recv_sem).wait()
    for k in range(n_plane):
        entries_ref[k : k + 1] = recv_b[k]
    whole(send_b.at[1:n_plane], b_send_sem).wait()


def finish(adj_from, entries_ref, adj_to, sens_to, sens, sems):
    copies = [
        pltpu.make_async_copy(adj_from.at[field], adj_to.at[field], sems.at[field]) for field in range(5)
    ]
    for copy in copies:
        copy.start()
    entries = entries_ref[...]
    slots = jnp.where(iota(entries.shape, 1) < 32, entries, 0.0)
    slots = slots + pltpu.roll(slots, 32, 1)
    slots = slots + pltpu.roll(slots, 64, 1)
    design = iota((E, E), 0).astype(F32)
    total = jnp.zeros((E, E), F32)
    for k in range(entries.shape[0]):
        total = total + jnp.where(slots[k : k + 1] == design, entries[k : k + 1], 0.0)
    terms = []
    for _ in range(3):
        term = total.astype(BF16)
        terms.append(term)
        total = total - term.astype(F32)
    coordinate = one_if(lax.shift_right_arithmetic(iota((16, E), 1), 5) == iota((16, E), 0) + 1).astype(BF16)
    sens[...] = mm_nt(jnp.concatenate([coordinate] * 3, 1), jnp.concatenate(terms, 1))[0:3]
    copies.append(pltpu.make_async_copy(sens, sens_to, sems.at[5]))
    copies[5].start()
    for copy in copies:
        copy.wait()


def on_device(sizes, *args):
    (psi, obj, u, metric, dt, visc, pen, fn, nf, fo, we, wf, wp, od, os_) = args
    row = lambda x: x.reshape(1, E)
    vmem = pl.BlockSpec(memory_space=pltpu.VMEM)
    hbm = pl.BlockSpec(memory_space=pltpu.HBM)
    n_span, n_chord, n_wall = sizes
    n_plane = n_chord * n_wall
    consts = tuple(jnp.asarray(t) for t in tables())
    results = pl.pallas_call(
        functools.partial(kernel, sizes),
        out_shape=(pltpu.VMEM((5, 125, E), F32), pltpu.VMEM((n_plane, E), F32)),
        in_specs=[hbm] * (15 + len(consts)),
        out_specs=(vmem, vmem),
        scratch_shapes=[
            *[pltpu.VMEM((1, E), F32)] * 3,
            pltpu.VMEM((6, E), F32),
            *[pltpu.VMEM((6, E), I32)] * 3,
            *[pltpu.VMEM((1, E), I32)] * 4,
            *[pltpu.VMEM(t.shape, BF16) for t in consts],
            pltpu.VMEM((5, 125, E), F32),
            pltpu.VMEM((5, 125, E), F32),
            pltpu.VMEM((5, 125, E), F32),
            pltpu.VMEM((3, 125, E), F32),
            pltpu.VMEM((3, 5, 32, E), F32),
            pltpu.VMEM((5, 128, E), F32),
            pltpu.VMEM((2, 128, 5 * E), BF16),
            pltpu.VMEM((320, 6 * E), BF16),
            pltpu.VMEM((256, 6 * E), BF16),
            pltpu.VMEM((6 * E, 6 * E), BF16),
            pltpu.VMEM((HALO * REQ, 6 * E), BF16),
            pltpu.VMEM((HALO, 1, E), F32),
            pltpu.VMEM((HALO, 1, E), F32),
            pltpu.VMEM((HALO, REQ, E), F32),
            pltpu.VMEM((HALO, REQ, E), F32),
            pltpu.VMEM((512, 5 * E), F32),
            pltpu.VMEM((512, E), F32),
            pltpu.VMEM((6 * E, 1024), BF16),
            pltpu.VMEM((160, 6 * E), F32),
            pltpu.VMEM((4, HALO * REQ, E), BF16),
            pltpu.VMEM((5, 128, E), F32),
            pltpu.VMEM((3, 128, 5 * E), F32),
            pltpu.VMEM((6 * E, E), BF16),
            pltpu.VMEM((4 * E, E), BF16),
            pltpu.VMEM((n_span, 1, E), F32),
            pltpu.VMEM((n_span, 1, E), F32),
            pltpu.VMEM((n_plane, 1, E), F32),
            pltpu.VMEM((n_plane, 1, E), F32),
            pltpu.SemaphoreType.DMA((15 + len(consts),)),
            *[pltpu.SemaphoreType.DMA] * 8,
            *[pltpu.SemaphoreType.REGULAR] * 3,
        ],
        compiler_params=pltpu.CompilerParams(
            collective_id=0, has_side_effects=True, vmem_limit_bytes=58 * 2**20
        ),
        name="adjoint_step",
    )(
        psi,
        obj,
        u,
        wp,
        row(metric),
        row(dt),
        row(visc),
        pen,
        fn,
        nf,
        fo,
        row(we),
        row(wf),
        row(od),
        row(os_),
        *consts,
    )
    return pl.pallas_call(
        finish,
        out_shape=(jax.ShapeDtypeStruct((5, 125, E), F32), jax.ShapeDtypeStruct((3, E), F32)),
        in_specs=[vmem] * 2,
        out_specs=(hbm, hbm),
        scratch_shapes=[pltpu.VMEM((3, E), F32), pltpu.SemaphoreType.DMA((6,))],
        compiler_params=pltpu.CompilerParams(vmem_limit_bytes=16 * 2**20),
        name="results",
    )(*results)


def solution(mesh):
    whole = P(None, None, AXES)
    plane = P(None, AXES)
    line = P(AXES)
    in_specs = (
        (whole,) * 3 + (line,) * 3 + (plane,) * 4 + (line,) * 2 + (whole, P(AXES, None), line)
    )
    sizes = tuple(mesh.shape[name] for name in AXES)
    return jax.shard_map(
        functools.partial(on_device, sizes),
        mesh=mesh,
        in_specs=in_specs,
        out_specs=(whole, plane),
        check_vma=False,
    )
```

```python
import functools
import math

import jax
import jax.numpy as jnp
import numpy as np
from jax import lax
from jax.experimental import pallas as pl
from jax.experimental.pallas import tpu as pltpu
from jax.sharding import PartitionSpec as P

AXES = ("span", "chord", "wall")
MESH = pl.DeviceIdType.MESH
F32 = jnp.float32
BF16 = jnp.bfloat16
I32 = jnp.int32
E = 128
REQ = 64
HALO = 5
OPPOSITE = (1, 0, 3, 2, 4)
G = 0.4


def derivative_table():
    points = [-1.0, -math.sqrt(3.0 / 7.0), 0.0, math.sqrt(3.0 / 7.0), 1.0]
    barycentric = []
    for i in range(5):
        product_value = 1.0
        for j in range(5):
            if j != i:
                product_value = product_value * (points[i] - points[j])
        barycentric.append(1.0 / product_value)
    matrix_values = np.zeros((5, 5))
    for i in range(5):
        for j in range(5):
            if j != i:
                matrix_values[i, j] = barycentric[j] / barycentric[i] / (points[i] - points[j])
        matrix_values[i, i] = -np.sum(matrix_values[i])
    return matrix_values


def face_node(face, a, b):
    edge = 0 if face % 2 == 0 else 4
    index = {0: (edge, a, b), 1: (a, edge, b), 2: (a, b, edge)}[face // 2]
    return 25 * index[0] + 5 * index[1] + index[2]


def oriented(orient, a, b):
    return {0: (a, b), 1: (b, a), 2: (4 - a, b), 3: (a, 4 - b)}[orient]


def split_table(table):
    high = table.astype(np.float32).astype(jnp.bfloat16)
    low = (table - high.astype(np.float64)).astype(np.float32).astype(jnp.bfloat16)
    return high, low


@functools.cache
def tables():
    d = derivative_table()
    eye = np.eye(5)
    ends = np.zeros((5, 5))
    ends[0, 0], ends[4, 4] = -0.5, 0.5
    along = [
        lambda m: np.kron(m, np.kron(eye, eye)),
        lambda m: np.kron(eye, np.kron(m, eye)),
        lambda m: np.kron(eye, np.kron(eye, m)),
    ]
    sweeps = np.zeros((512, 128))
    for axis in range(3):
        sweeps[128 * axis : 128 * axis + 125, :125] = along[axis](d.T + ends)
        sweeps[384:509, :125] += along[axis](d) @ along[axis](d.T)
    sweep_high, sweep_low = split_table(sweeps)
    traces = np.zeros((192, 128))
    to_nodes = np.zeros((3, 128, 128))
    turns = np.zeros((160, 512))
    penalties = np.zeros((512, 32))
    for face in range(6):
        axis, sign = face // 2, (1.0 if face % 2 else -1.0)
        for a in range(5):
            for b in range(5):
                node = face_node(face, a, b)
                traces[32 * face + 5 * a + b, node] = 1.0
                for term in range(3):
                    penalties[128 * axis + node, 8 * term + face] = 2.0 * sign
                    penalties[384 + node, 8 * term + face] = 1.0
                for term in range(2):
                    to_nodes[axis, node, 64 * term + 32 * (face % 2) + 5 * a + b] = 0.5 * sign
    dense = np.zeros((128, 160))
    for field in range(5):
        for ab in range(25):
            dense[25 * field + ab, 32 * field + ab] = 1.0
            for orient in range(4):
                oa, ob = oriented(orient, ab // 5, ab % 5)
                turns[32 * field + ab, 128 * orient + 25 * field + 5 * oa + ob] = 1.0
    as_bf16 = lambda t: t.astype(np.float32).astype(jnp.bfloat16)
    return (
        np.concatenate([sweep_high, sweep_low], 0),
        as_bf16(traces),
        as_bf16(to_nodes),
        as_bf16(penalties),
        as_bf16(dense),
        as_bf16(turns),
    )


def split(x):
    high = x.astype(BF16)
    return high, (x - high.astype(F32)).astype(BF16)


def mm(a, b):
    return lax.dot_general(a, b, (((1,), (0,)), ((), ())), preferred_element_type=F32)


def mm_nt(a, b):
    return lax.dot_general(a, b, (((1,), (1,)), ((), ())), preferred_element_type=F32)


def iota(shape, dim):
    return lax.broadcasted_iota(I32, shape, dim)


def one_if(condition):
    return jnp.where(condition, 1.0, 0.0)


def ring_steps(k, n):
    return min(k, n - k)


def far_first(n_span, n_chord):
    offsets = [(a, b) for a in range(n_span) for b in range(n_chord) if a or b]
    steps = lambda o: ring_steps(o[0] // 4, 4) + ring_steps(o[0] % 4, 4) + ring_steps(o[1], n_chord)
    return sorted(offsets, key=lambda o: -steps(o))


def whole(ref, sem):
    return pltpu.make_async_copy(ref, ref, sem)


def kernel(
    sizes,
    psi_hbm,
    obj_hbm,
    u_hbm,
    wp_hbm,
    metric_hbm,
    dt_hbm,
    visc_hbm,
    pen_hbm,
    fn_hbm,
    nf_hbm,
    fo_hbm,
    we_hbm,
    wf_hbm,
    od_hbm,
    os_hbm,
    sweeps_hbm,
    traces_hbm,
    to_nodes_hbm,
    penalties_hbm,
    dense_hbm,
    turns_hbm,
    adj_out,
    entries_ref,
    metric_ref,
    dt_ref,
    visc_ref,
    pen_ref,
    fn_ref,
    nf_ref,
    fo_ref,
    we_ref,
    wf_ref,
    od_ref,
    os_ref,
    sweeps_ref,
    traces_ref,
    to_nodes_ref,
    penalties_ref,
    dense_ref,
    turns_ref,
    psi,
    obj,
    u,
    wp,
    wpad,
    adj,
    psib,
    xp,
    xd,
    local_hot,
    request_hot,
    req_out,
    req_in,
    resp_out,
    resp_in,
    swept,
    pen_nodes,
    local_turned,
    near,
    far_masks,
    state,
    jump,
    wall_hot,
    to_chip,
    owner_out,
    owner_in,
    values_out,
    values_in,
    send_all,
    in_sem,
    req_send_sem,
    req_recv_sem,
    resp_send_sem,
    resp_recv_sem,
    owner_send_sem,
    owner_recv_sem,
    values_send_sem,
    values_recv_sem,
    all_send_sem,
    all_recv_sem,
    round2_sem,
    round3_sem,
    round4_sem,
):
    n_span, n_chord, n_wall = sizes
    n_plane = n_chord * n_wall
    s, c, w = (lax.axis_index(name) for name in AXES)
    part = (s * n_chord + c) * n_wall + w

    sources = {
        "fn": (fn_hbm, fn_ref),
        "nf": (nf_hbm, nf_ref),
        "psi": (psi_hbm, psi),
        "traces": (traces_hbm, traces_ref),
        "dense": (dense_hbm, dense_ref),
        "od": (od_hbm, od_ref),
        "sweeps": (sweeps_hbm, sweeps_ref),
        "fo": (fo_hbm, fo_ref),
        "pen": (pen_hbm, pen_ref),
        "dt": (dt_hbm, dt_ref),
        "penalties": (penalties_hbm, penalties_ref),
        "we": (we_hbm, we_ref),
        "wf": (wf_hbm, wf_ref),
        "wp": (wp_hbm, wp),
        "os": (os_hbm, os_ref),
        "turns": (turns_hbm, turns_ref),
        "to_nodes": (to_nodes_hbm, to_nodes_ref),
        "u": (u_hbm, u),
        "obj": (obj_hbm, obj),
        "metric": (metric_hbm, metric_ref),
        "visc": (visc_hbm, visc_ref),
    }
    loads = {}
    for i, (name, (src, dst)) in enumerate(sources.items()):
        loads[name] = pltpu.make_async_copy(src, dst, in_sem.at[i])
    first = ("fn", "nf", "psi", "traces", "dense")
    for name in first:
        loads[name].start()

    def ready(*names):
        for name in names:
            loads[name].wait()

    barrier = pltpu.get_barrier_semaphore()
    def along(ds, dc, other=False):
        return (
            jnp.bitwise_and(s + ds, n_span - 1),
            jnp.bitwise_and(c + dc, n_chord - 1),
            1 - w if other else w,
        )

    nearest = (along(1, 0), along(-1, 0), along(4, 0), along(-4, 0), along(0, 1), along(0, -1), along(0, 0, True))

    def greet(sem, peers):
        for peer in peers:
            pl.semaphore_signal(sem, inc=1, device_id=peer, device_id_type=MESH)

    greet(barrier, nearest)
    for name in sources:
        if name not in first:
            loads[name].start()

    ready("fn", "nf")
    fn, nf = fn_ref[...], nf_ref[...]
    offset = jnp.where(fn >= 0, lax.shift_right_arithmetic(fn, 7) - part, 1 << 20)
    elem = jnp.bitwise_and(fn, E - 1)
    slot = iota((8, E), 0)
    wanted = jnp.where(slot == 4, 1 - 2 * w, 1 << 21)
    for j, step in enumerate((-n_plane, n_plane, -n_wall, n_wall)):
        wanted = jnp.where(slot == j, step, wanted)
    named = [offset[f : f + 1] == wanted for f in range(6)]
    before = jnp.concatenate(
        [one_if(iota((E, E), 0) < iota((E, E), 1)), jnp.ones((E, E), F32)], 1
    ).astype(BF16)
    counts = mm(jnp.concatenate([one_if(m) for m in named], 0).astype(BF16), before)
    base = jnp.zeros((8, E), F32)
    place = iota((REQ, E), 0).astype(F32)
    sub16 = iota((16, E), 0)
    codes = []
    for f in range(6):
        rank = jnp.where(named[f], counts[8 * f : 8 * f + 8, :E] + base, -1.0)
        base = base + counts[8 * f : 8 * f + 8, E:]
        for j in range(HALO):
            request_hot[REQ * j : REQ * (j + 1), E * f : E * (f + 1)] = one_if(
                rank[j : j + 1] == place
            ).astype(BF16)
        code = jnp.where(
            sub16 == 0, elem[f : f + 1], jnp.where(sub16 == 1, nf[f : f + 1], (sub16 == 2).astype(I32))
        )
        codes.append(code.astype(F32).astype(BF16))
    codes = jnp.concatenate(codes, 1)
    for j in range(HALO):
        got = mm_nt(codes, request_hot[REQ * j : REQ * (j + 1), :])
        req_out[j] = jnp.zeros((1, E), F32)
        req_out[j, :, 0:REQ] = got[0:1] + 128.0 * got[1:2] + 2048.0 * (1.0 - got[2:3])

    pl.semaphore_wait(barrier, 7)
    beside = (along(-1, 0), along(1, 0), along(0, -1), along(0, 1), along(0, 0, True))
    requests = [
        pltpu.make_async_remote_copy(
            src_ref=req_out.at[j],
            dst_ref=req_in.at[OPPOSITE[j]],
            send_sem=req_send_sem,
            recv_sem=req_recv_sem,
            device_id=beside[j],
            device_id_type=MESH,
        )
        for j in range(HALO)
    ]
    for copy in requests:
        copy.start()
    greet(round2_sem, nearest)
    ready("od")
    owner = od_ref[...]
    owner_out[...] = owner.astype(F32)
    owner_copy = pltpu.make_async_remote_copy(
        src_ref=owner_out,
        dst_ref=owner_in,
        send_sem=owner_send_sem,
        recv_sem=owner_recv_sem,
        device_id=beside[4],
        device_id_type=MESH,
    )
    owner_copy.start()

    ready("psi", "traces", "dense")
    for field in range(5):
        psib[0, 112:128, E * field : E * (field + 1)] = jnp.zeros((16, E), BF16)
        psib[1, 112:128, E * field : E * (field + 1)] = jnp.zeros((16, E), BF16)
        high, low = split(psi[field])
        psib[0, 0:125, E * field : E * (field + 1)] = high
        psib[1, 0:125, E * field : E * (field + 1)] = low
    for half in range(2):
        got = mm(traces_ref[...], psib[half]).astype(BF16)
        for field in range(5):
            for f in range(6):
                xp[160 * half + 32 * field : 160 * half + 32 * (field + 1), E * f : E * (f + 1)] = got[
                    32 * f : 32 * (f + 1), E * field : E * (field + 1)
                ]
        xd[128 * half : 128 * (half + 1), :] = mm(
            dense_ref[...], xp[160 * half : 160 * (half + 1), :]
        ).astype(BF16)

    slots8 = iota((8, E), 0)
    mine = jnp.full((8, E), -1, I32)
    for f in range(6):
        code = jnp.where(offset[f : f + 1] == 0, elem[f : f + 1] + E * nf[f : f + 1], -1)
        mine = jnp.where(slots8 == f, code, mine)
    ready("fo")
    fo = fo_ref[...]
    turned = jnp.concatenate(
        [mine.astype(F32), fo.astype(F32), jnp.zeros((E - 14, E), F32)], 0
    ).T
    columns = iota((E, 6 * E), 1).astype(F32)
    for f in range(6):
        local_hot[E * f : E * (f + 1), :] = one_if(turned[:, f : f + 1] == columns).astype(BF16)
    ready("sweeps", "pen", "penalties", "dt")
    swept[...] = (
        mm(sweeps_ref[0:512], psib[0]) + mm(sweeps_ref[512:1024], psib[0]) + mm(sweeps_ref[0:512], psib[1])
    )
    pen8 = jnp.concatenate([pen_ref[...], jnp.zeros((2, E), F32)], 0)
    pen_terms = []
    for _ in range(3):
        pen_high = pen8.astype(BF16).astype(F32)
        pen_terms.append(pen_high)
        pen8 = pen8 - pen_high
    pen_terms.append(jnp.zeros((8, E), F32))
    pen_nodes[...] = dt_ref[...] * mm(penalties_ref[...], jnp.concatenate(pen_terms, 0).astype(BF16))

    own_answers = mm_nt(local_hot[...], xd[...]).astype(BF16)
    for f in range(6):
        seen = jnp.broadcast_to(turned[:, 8 + f : 9 + f], (E, E))
        for o in range(4):
            mask = one_if(seen == o).astype(BF16)
            for half in range(2):
                local_turned[E * f : E * (f + 1), 512 * half + E * o : 512 * half + E * (o + 1)] = (
                    own_answers[E * f : E * (f + 1), E * half : E * (half + 1)] * mask
                )
    ready("turns")
    turns2 = jnp.concatenate([turns_ref[...], turns_ref[...]], 1)
    near[...] = mm_nt(turns2, local_turned[...])
    whole(req_in, req_recv_sem).wait()
    pl.semaphore_wait(round2_sem, 7)
    greet(round3_sem, (along(0, 1), along(0, -1), along(5, 0), along(-5, 0)))
    asked = jnp.zeros((8, E), F32)
    for j in range(HALO):
        asked = jnp.where(slots8 == j, req_in[j], asked)
    asked = jnp.concatenate([asked, jnp.zeros((E - 8, E), F32)], 0).T
    columns = iota((REQ, 6 * E), 1).astype(F32)
    for j in range(HALO):
        hot = one_if(asked[0:REQ, j : j + 1] == columns).astype(BF16)
        got = mm_nt(hot, xd[...])
        resp_out[j] = got[:, :E] + got[:, E:]
        copy = pltpu.make_async_remote_copy(
            src_ref=resp_out.at[j],
            dst_ref=resp_in.at[OPPOSITE[j]],
            send_sem=resp_send_sem,
            recv_sem=resp_recv_sem,
            device_id=beside[j],
            device_id_type=MESH,
        )
        copy.start()

    views = jnp.concatenate(
        [jnp.broadcast_to(fo[f : f + 1], (16, E)).astype(F32).astype(BF16) for f in range(6)], 1
    )
    views = mm_nt(request_hot[...], jnp.concatenate([views] * 8, 0))
    for o in range(4):
        far_masks[o] = one_if(views == o).astype(BF16)

    ready("we", "wf", "wp", "os")
    wall_code = we_ref[...] + E * wf_ref[...]
    for g in range(6):
        wall_hot[E * g : E * (g + 1), :] = one_if(wall_code == iota((E, E), 0) + E * g).astype(BF16)
    for x in range(3):
        for field in range(5):
            wpad[x, field] = jnp.zeros((32, E), F32)
            wpad[x, field, 0:25] = wp[x, 25 * field : 25 * (field + 1)]
    owner_rows = jnp.broadcast_to(owner.astype(F32), (E, E))
    earlier = one_if((owner_rows == owner_rows.T) & (iota((E, E), 0) < iota((E, E), 1)))
    rank = jnp.sum(earlier, axis=0, keepdims=True)
    owner_copy.wait_recv()
    for half, named_owner in enumerate((owner, owner_in[...].astype(I32))):
        chip = lax.shift_right_arithmetic(named_owner, n_wall.bit_length() - 1)
        here = jnp.bitwise_and(named_owner, n_wall - 1) == w
        to_chip[:, E * half : E * (half + 1)] = one_if(jnp.where(here, chip, -1) == iota((E, E), 0)).astype(BF16)

    pl.semaphore_wait(round3_sem, 4)
    greet(round4_sem, (along(0, 3), along(0, -3)))
    ready("u", "obj", "metric", "visc")
    metric, dt, visc = metric_ref[...], dt_ref[...], visc_ref[...]
    dt_metric, dt_visc = dt * metric, dt * visc

    def lanes(field):
        return slice(E * field, E * (field + 1))

    def transposed_flux(axes, vel, kinetic, enthalpy, weights):
        out = [0.0] * 5
        a_sum = 0.0
        for axis in axes:
            wd, vd = weights[axis], vel[axis]
            carried = wd[1] * vel[0] + wd[2] * vel[1] + wd[3] * vel[2] + enthalpy * wd[4]
            a_sum = a_sum + (wd[1 + axis] + vd * wd[4])
            out[0] = out[0] - vd * carried
            for i in range(3):
                out[1 + i] = out[1 + i] + vd * wd[1 + i]
            out[1 + axis] = out[1 + axis] + (wd[0] + carried)
            out[4] = out[4] + vd * wd[4]
        ga = G * a_sum
        out[0] = out[0] + kinetic * ga
        for i in range(3):
            out[1 + i] = out[1 + i] - vel[i] * ga
        out[4] = out[4] + ga
        return out

    for start in range(0, 125, 8):
        stop = min(start + 8, 125)
        cut = slice(start, stop)
        rho, m1, m2, m3, energy = (u[field, cut] for field in range(5))
        inverse = 1.0 / rho
        vel = (m1 * inverse, m2 * inverse, m3 * inverse)
        kinetic = 0.5 * (vel[0] * vel[0] + vel[1] * vel[1] + vel[2] * vel[2])
        pressure = G * (energy - rho * kinetic)
        enthalpy = (energy + pressure) * inverse
        for i, kept in enumerate((*vel, kinetic, enthalpy)):
            state[i, cut] = kept
        weights = [
            [swept[128 * axis + start : 128 * axis + stop, lanes(field)] for field in range(5)]
            for axis in range(3)
        ]
        out = transposed_flux(range(3), vel, kinetic, enthalpy, weights)
        pen = 1.0 - pen_nodes[384 + start : 384 + stop]
        for field in range(5):
            adj[field, cut] = (
                pen * psi[field, cut]
                + dt * obj[field, cut]
                - dt_metric * out[field]
                - dt_visc * swept[384 + start : 384 + stop, lanes(field)]
            )
    for field in range(5):
        adj[field, 125:128] = jnp.zeros((3, E), F32)
    ready("to_nodes")

    whole(resp_in, resp_recv_sem).wait()
    answered = jnp.concatenate([resp_in[j] for j in range(HALO)], 0)
    answered = split(answered)
    placed = []
    for half in range(2):
        masked = jnp.concatenate([answered[half] * far_masks[o] for o in range(4)], 1)
        placed.append(mm_nt(turns_ref[...], masked).astype(BF16))
    far = mm(jnp.concatenate(placed, 0), request_hot[...])
    trace = split(near[...] + (far[:160] + far[160:]))
    for axis in range(3):
        rhs = jnp.concatenate(
            [
                jnp.concatenate(
                    [
                        trace[half][32 * field : 32 * (field + 1), E * f : E * (f + 1)]
                        for half in range(2)
                        for f in (2 * axis, 2 * axis + 1)
                    ],
                    0,
                )
                for field in range(5)
            ],
            1,
        )
        jump[axis] = mm(to_nodes_ref[axis], rhs)

    for start in range(0, 125, 8):
        stop = min(start + 8, 125)
        cut = slice(start, stop)
        axes = range(3) if start < 25 or stop > 100 else range(1, 3)
        vel = tuple(state[i, cut] for i in range(3))
        weights = [[jump[axis, cut, lanes(field)] for field in range(5)] for axis in range(3)]
        out = transposed_flux(axes, vel, state[3, cut], state[4, cut], weights)
        for field in range(5):
            new = adj[field, cut] - dt_metric * out[field]
            for axis in axes:
                new = new + pen_nodes[128 * axis + start : 128 * axis + stop] * weights[axis][field]
            adj[field, cut] = new
            adj_out[field, cut] = new

    for field in range(5):
        high, low = split(adj[field])
        psib[0, :, E * field : E * (field + 1)] = high
        psib[1, :, E * field : E * (field + 1)] = low
    for half in range(2):
        got = mm(traces_ref[...], psib[half]).astype(BF16)
        for field in range(5):
            for f in range(6):
                xp[160 * half + 32 * field : 160 * half + 32 * (field + 1), E * f : E * (f + 1)] = got[
                    32 * f : 32 * (f + 1), E * field : E * (field + 1)
                ]
    taken = mm(xp[...], wall_hot[...])
    taken = taken[:160] + taken[160:]
    values = [os_ref[...].astype(F32)]
    for x in range(3):
        total = wpad[x, 0] * taken[0:32]
        for field in range(1, 5):
            total = total + wpad[x, field] * taken[32 * field : 32 * (field + 1)]
        values.append(jnp.sum(total, axis=0, keepdims=True))
    mine = jnp.concatenate(values + values, 0)
    mine = jnp.where(rank == lax.shift_right_arithmetic(slots8, 2).astype(F32), mine, 0.0)
    values_out[...] = mine
    values_copy = pltpu.make_async_remote_copy(
        src_ref=values_out,
        dst_ref=values_in,
        send_sem=values_send_sem,
        recv_sem=values_recv_sem,
        device_id=beside[4],
        device_id_type=MESH,
    )
    values_copy.start()
    nothing = jnp.zeros((8, E), F32)
    rest = jnp.zeros((E - 16, 2 * E), BF16)
    values_copy.wait_recv()
    both = jnp.concatenate(
        [jnp.concatenate([mine, nothing], 0), jnp.concatenate([nothing, values_in[...]], 0)], 1
    )
    terms = []
    for _ in range(3):
        term = both.astype(BF16)
        terms.append(jnp.concatenate([term, rest], 0))
        both = both - term.astype(F32)
    sent = mm_nt(jnp.concatenate([to_chip[...]] * 3, 1), jnp.concatenate(terms, 1))
    for k in range(n_span * n_chord):
        send_all[k] = sent[k : k + 1]
    pl.semaphore_wait(round4_sem, 2)
    for k, (ds, dc) in enumerate(far_first(n_span, n_chord)):
        there = along(ds, dc)
        pltpu.make_async_remote_copy(
            src_ref=send_all.at[there[0] * n_chord + there[1]],
            dst_ref=entries_ref.at[k + 1],
            send_sem=all_send_sem,
            recv_sem=all_recv_sem,
            device_id=there,
            device_id_type=MESH,
        ).start()
    entries_ref[0] = send_all[s * n_chord + c]
    whole(req_out, req_send_sem).wait()
    whole(resp_out, resp_send_sem).wait()
    owner_copy.wait_send()
    values_copy.wait_send()
    whole(entries_ref.at[1 : n_span * n_chord], all_recv_sem).wait()
    whole(send_all.at[1 : n_span * n_chord], all_send_sem).wait()


def finish(adj_from, entries_ref, adj_to, sens_to, sens, sems):
    copies = [
        pltpu.make_async_copy(adj_from.at[field], adj_to.at[field], sems.at[field]) for field in range(5)
    ]
    for copy in copies:
        copy.start()
    entries = entries_ref[...].reshape(entries_ref.shape[0], E)
    if entries.shape[0] < E:
        entries = jnp.concatenate([entries, jnp.zeros((E - entries.shape[0], E), F32)], 0)
    entries = entries.T
    design = iota((E, E), 0).astype(F32)
    both = jnp.concatenate([entries[0:8], entries[8:16]], 1)
    terms = []
    for _ in range(3):
        term = both.astype(BF16).astype(F32)
        terms.append(term)
        both = both - term
    terms = jnp.concatenate(terms, 0).astype(BF16)
    total = jnp.zeros((3, E), F32)
    for r in range(2):
        hot = jnp.concatenate(
            [one_if(entries[8 * g + 4 * r : 8 * g + 4 * r + 1] == design).astype(BF16) for g in range(2)], 1
        )
        got = mm_nt(terms, hot)
        got = got[0:8] + got[8:16] + got[16:24]
        total = total + got[4 * r + 1 : 4 * r + 4]
    sens[...] = total
    copies.append(pltpu.make_async_copy(sens, sens_to, sems.at[5]))
    copies[5].start()
    for copy in copies:
        copy.wait()


def on_device(sizes, *args):
    (psi, obj, u, metric, dt, visc, pen, fn, nf, fo, we, wf, wp, od, os_) = args
    row = lambda x: x.reshape(1, E)
    vmem = pl.BlockSpec(memory_space=pltpu.VMEM)
    hbm = pl.BlockSpec(memory_space=pltpu.HBM)
    n_span, n_chord, n_wall = sizes
    n_chips = n_span * n_chord
    consts = tuple(jnp.asarray(t) for t in tables())
    results = pl.pallas_call(
        functools.partial(kernel, sizes),
        out_shape=(pltpu.VMEM((5, 125, E), F32), pltpu.VMEM((n_chips, 1, E), F32)),
        in_specs=[hbm] * (15 + len(consts)),
        out_specs=(vmem, vmem),
        scratch_shapes=[
            *[pltpu.VMEM((1, E), F32)] * 3,
            pltpu.VMEM((6, E), F32),
            *[pltpu.VMEM((6, E), I32)] * 3,
            *[pltpu.VMEM((1, E), I32)] * 4,
            *[pltpu.VMEM(t.shape, BF16) for t in consts],
            pltpu.VMEM((5, 125, E), F32),
            pltpu.VMEM((5, 125, E), F32),
            pltpu.VMEM((5, 125, E), F32),
            pltpu.VMEM((3, 125, E), F32),
            pltpu.VMEM((3, 5, 32, E), F32),
            pltpu.VMEM((5, 128, E), F32),
            pltpu.VMEM((2, 128, 5 * E), BF16),
            pltpu.VMEM((320, 6 * E), BF16),
            pltpu.VMEM((256, 6 * E), BF16),
            pltpu.VMEM((6 * E, 6 * E), BF16),
            pltpu.VMEM((HALO * REQ, 6 * E), BF16),
            pltpu.VMEM((HALO, 1, E), F32),
            pltpu.VMEM((HALO, 1, E), F32),
            pltpu.VMEM((HALO, REQ, E), F32),
            pltpu.VMEM((HALO, REQ, E), F32),
            pltpu.VMEM((512, 5 * E), F32),
            pltpu.VMEM((512, E), F32),
            pltpu.VMEM((6 * E, 1024), BF16),
            pltpu.VMEM((160, 6 * E), F32),
            pltpu.VMEM((4, HALO * REQ, E), BF16),
            pltpu.VMEM((5, 128, E), F32),
            pltpu.VMEM((3, 128, 5 * E), F32),
            pltpu.VMEM((6 * E, E), BF16),
            pltpu.VMEM((E, 2 * E), BF16),
            pltpu.VMEM((1, E), F32),
            pltpu.VMEM((1, E), F32),
            pltpu.VMEM((8, E), F32),
            pltpu.VMEM((8, E), F32),
            pltpu.VMEM((n_chips, 1, E), F32),
            pltpu.SemaphoreType.DMA((15 + len(consts),)),
            *[pltpu.SemaphoreType.DMA] * 10,
            *[pltpu.SemaphoreType.REGULAR] * 3,
        ],
        compiler_params=pltpu.CompilerParams(
            collective_id=0, has_side_effects=True, vmem_limit_bytes=58 * 2**20
        ),
        name="adjoint_step",
    )(
        psi,
        obj,
        u,
        wp,
        row(metric),
        row(dt),
        row(visc),
        pen,
        fn,
        nf,
        fo,
        row(we),
        row(wf),
        row(od),
        row(os_),
        *consts,
    )
    return pl.pallas_call(
        finish,
        out_shape=(jax.ShapeDtypeStruct((5, 125, E), F32), jax.ShapeDtypeStruct((3, E), F32)),
        in_specs=[vmem] * 2,
        out_specs=(hbm, hbm),
        scratch_shapes=[pltpu.VMEM((3, E), F32), pltpu.SemaphoreType.DMA((6,))],
        compiler_params=pltpu.CompilerParams(vmem_limit_bytes=16 * 2**20),
        name="results",
    )(*results)


def solution(mesh):
    whole = P(None, None, AXES)
    plane = P(None, AXES)
    line = P(AXES)
    in_specs = (
        (whole,) * 3 + (line,) * 3 + (plane,) * 4 + (line,) * 2 + (whole, P(AXES, None), line)
    )
    sizes = tuple(mesh.shape[name] for name in AXES)
    return jax.shard_map(
        functools.partial(on_device, sizes),
        mesh=mesh,
        in_specs=in_specs,
        out_specs=(whole, plane),
        check_vma=False,
    )
```

```python
import functools
import itertools
import math

import jax
import jax.numpy as jnp
import numpy as np
from jax import lax
from jax.experimental import pallas as pl
from jax.experimental.pallas import tpu as pltpu
from jax.sharding import PartitionSpec as P

AXES = ("span", "chord", "wall")
MESH = pl.DeviceIdType.MESH
F32 = jnp.float32
BF16 = jnp.bfloat16
I32 = jnp.int32
E = 128
REQ = 64
HALO = 5
OPPOSITE = (1, 0, 3, 2, 4)
G = 0.4


def derivative_table():
    points = [-1.0, -math.sqrt(3.0 / 7.0), 0.0, math.sqrt(3.0 / 7.0), 1.0]
    barycentric = []
    for i in range(5):
        product_value = 1.0
        for j in range(5):
            if j != i:
                product_value = product_value * (points[i] - points[j])
        barycentric.append(1.0 / product_value)
    matrix_values = np.zeros((5, 5))
    for i in range(5):
        for j in range(5):
            if j != i:
                matrix_values[i, j] = barycentric[j] / barycentric[i] / (points[i] - points[j])
        matrix_values[i, i] = -np.sum(matrix_values[i])
    return matrix_values


def face_node(face, a, b):
    edge = 0 if face % 2 == 0 else 4
    index = {0: (edge, a, b), 1: (a, edge, b), 2: (a, b, edge)}[face // 2]
    return 25 * index[0] + 5 * index[1] + index[2]


def oriented(orient, a, b):
    return {0: (a, b), 1: (b, a), 2: (4 - a, b), 3: (a, 4 - b)}[orient]


def split_table(table):
    high = table.astype(np.float32).astype(jnp.bfloat16)
    low = (table - high.astype(np.float64)).astype(np.float32).astype(jnp.bfloat16)
    return high, low


@functools.cache
def tables():
    d = derivative_table()
    eye = np.eye(5)
    ends = np.zeros((5, 5))
    ends[0, 0], ends[4, 4] = -0.5, 0.5
    along = [
        lambda m: np.kron(m, np.kron(eye, eye)),
        lambda m: np.kron(eye, np.kron(m, eye)),
        lambda m: np.kron(eye, np.kron(eye, m)),
    ]
    sweeps = np.zeros((512, 128))
    for axis in range(3):
        sweeps[128 * axis : 128 * axis + 125, :125] = along[axis](d.T + ends)
        sweeps[384:509, :125] += along[axis](d) @ along[axis](d.T)
    sweep_high, sweep_low = split_table(sweeps)
    traces = np.zeros((192, 128))
    to_nodes = np.zeros((3, 128, 128))
    turns = np.zeros((160, 512))
    penalties = np.zeros((512, 32))
    for face in range(6):
        axis, sign = face // 2, (1.0 if face % 2 else -1.0)
        for a in range(5):
            for b in range(5):
                node = face_node(face, a, b)
                traces[32 * face + 5 * a + b, node] = 1.0
                for term in range(3):
                    penalties[128 * axis + node, 8 * term + face] = 2.0 * sign
                    penalties[384 + node, 8 * term + face] = 1.0
                for term in range(2):
                    to_nodes[axis, node, 64 * term + 32 * (face % 2) + 5 * a + b] = 0.5 * sign
    dense = np.zeros((128, 160))
    for field in range(5):
        for ab in range(25):
            dense[25 * field + ab, 32 * field + ab] = 1.0
            for orient in range(4):
                oa, ob = oriented(orient, ab // 5, ab % 5)
                turns[32 * field + ab, 128 * orient + 25 * field + 5 * oa + ob] = 1.0
    as_bf16 = lambda t: t.astype(np.float32).astype(jnp.bfloat16)
    return (
        np.concatenate([sweep_high, sweep_low], 0),
        as_bf16(traces),
        as_bf16(to_nodes),
        as_bf16(penalties),
        as_bf16(dense),
        as_bf16(turns),
    )


def split(x):
    high = x.astype(BF16)
    return high, (x - high.astype(F32)).astype(BF16)


def mm(a, b):
    return lax.dot_general(a, b, (((1,), (0,)), ((), ())), preferred_element_type=F32)


def mm_nt(a, b):
    return lax.dot_general(a, b, (((1,), (1,)), ((), ())), preferred_element_type=F32)


def iota(shape, dim):
    return lax.broadcasted_iota(I32, shape, dim)


def one_if(condition):
    return jnp.where(condition, 1.0, 0.0)


def ring_steps(k, n):
    return min(k, n - k)


def far_first(n_span, n_chord, n_wall):
    rows = max(n_span // 4, 1)
    wide = n_span // rows
    sizes = (rows, wide, n_chord, n_wall)
    offsets = [o for o in itertools.product(*map(range, sizes)) if any(o)]
    steps = lambda o: sum(ring_steps(k, n) for k, n in zip(o[:3], sizes)) + 0.1 * o[3]
    return sorted(offsets, key=lambda o: -steps(o))


def whole(ref, sem):
    return pltpu.make_async_copy(ref, ref, sem)


def kernel(
    sizes,
    psi_hbm,
    obj_hbm,
    u_hbm,
    wp_hbm,
    metric_hbm,
    dt_hbm,
    visc_hbm,
    pen_hbm,
    fn_hbm,
    nf_hbm,
    fo_hbm,
    we_hbm,
    wf_hbm,
    od_hbm,
    os_hbm,
    sweeps_hbm,
    traces_hbm,
    to_nodes_hbm,
    penalties_hbm,
    dense_hbm,
    turns_hbm,
    adj_out,
    entries_ref,
    metric_ref,
    dt_ref,
    visc_ref,
    pen_ref,
    fn_ref,
    nf_ref,
    fo_ref,
    we_ref,
    wf_ref,
    od_ref,
    os_ref,
    sweeps_ref,
    traces_ref,
    to_nodes_ref,
    penalties_ref,
    dense_ref,
    turns_ref,
    psi,
    obj,
    u,
    wp,
    wpad,
    adj,
    psib,
    xp,
    xd,
    local_hot,
    request_hot,
    req_out,
    req_in,
    resp_out,
    resp_in,
    swept,
    pen_nodes,
    local_turned,
    near,
    far_masks,
    state,
    jump,
    wall_hot,
    to_owner,
    send_all,
    in_sem,
    req_send_sem,
    req_recv_sem,
    resp_send_sem,
    resp_recv_sem,
    all_send_sem,
    all_recv_sem,
    round2_sem,
    round3_sem,
    round4_sem,
):
    n_span, n_chord, n_wall = sizes
    n_plane = n_chord * n_wall
    s, c, w = (lax.axis_index(name) for name in AXES)
    part = (s * n_chord + c) * n_wall + w

    sources = {
        "fn": (fn_hbm, fn_ref),
        "nf": (nf_hbm, nf_ref),
        "psi": (psi_hbm, psi),
        "traces": (traces_hbm, traces_ref),
        "dense": (dense_hbm, dense_ref),
        "od": (od_hbm, od_ref),
        "sweeps": (sweeps_hbm, sweeps_ref),
        "fo": (fo_hbm, fo_ref),
        "pen": (pen_hbm, pen_ref),
        "dt": (dt_hbm, dt_ref),
        "penalties": (penalties_hbm, penalties_ref),
        "we": (we_hbm, we_ref),
        "wf": (wf_hbm, wf_ref),
        "wp": (wp_hbm, wp),
        "os": (os_hbm, os_ref),
        "turns": (turns_hbm, turns_ref),
        "to_nodes": (to_nodes_hbm, to_nodes_ref),
        "u": (u_hbm, u),
        "obj": (obj_hbm, obj),
        "metric": (metric_hbm, metric_ref),
        "visc": (visc_hbm, visc_ref),
    }
    loads = {}
    for i, (name, (src, dst)) in enumerate(sources.items()):
        loads[name] = pltpu.make_async_copy(src, dst, in_sem.at[i])
    first = ("fn", "nf", "psi", "traces", "dense")
    for name in first:
        loads[name].start()

    def ready(*names):
        for name in names:
            loads[name].wait()

    barrier = pltpu.get_barrier_semaphore()
    def along(ds, dc, other=False):
        return (
            jnp.bitwise_and(s + ds, n_span - 1),
            jnp.bitwise_and(c + dc, n_chord - 1),
            1 - w if other else w,
        )

    nearest = (along(1, 0), along(-1, 0), along(4, 0), along(-4, 0), along(0, 1), along(0, -1), along(0, 0, True))

    def greet(sem, peers):
        for peer in peers:
            pl.semaphore_signal(sem, inc=1, device_id=peer, device_id_type=MESH)

    greet(barrier, nearest)
    for name in sources:
        if name not in first:
            loads[name].start()

    ready("fn", "nf")
    fn, nf = fn_ref[...], nf_ref[...]
    offset = jnp.where(fn >= 0, lax.shift_right_arithmetic(fn, 7) - part, 1 << 20)
    elem = jnp.bitwise_and(fn, E - 1)
    slot = iota((8, E), 0)
    wanted = jnp.where(slot == 4, 1 - 2 * w, 1 << 21)
    for j, step in enumerate((-n_plane, n_plane, -n_wall, n_wall)):
        wanted = jnp.where(slot == j, step, wanted)
    named = [offset[f : f + 1] == wanted for f in range(6)]
    before = jnp.concatenate(
        [one_if(iota((E, E), 0) < iota((E, E), 1)), jnp.ones((E, E), F32)], 1
    ).astype(BF16)
    counts = mm(jnp.concatenate([one_if(m) for m in named], 0).astype(BF16), before)
    base = jnp.zeros((8, E), F32)
    place = iota((REQ, E), 0).astype(F32)
    sub16 = iota((16, E), 0)
    codes = []
    for f in range(6):
        rank = jnp.where(named[f], counts[8 * f : 8 * f + 8, :E] + base, -1.0)
        base = base + counts[8 * f : 8 * f + 8, E:]
        for j in range(HALO):
            request_hot[REQ * j : REQ * (j + 1), E * f : E * (f + 1)] = one_if(
                rank[j : j + 1] == place
            ).astype(BF16)
        code = jnp.where(
            sub16 == 0, elem[f : f + 1], jnp.where(sub16 == 1, nf[f : f + 1], (sub16 == 2).astype(I32))
        )
        codes.append(code.astype(F32).astype(BF16))
    codes = jnp.concatenate(codes, 1)
    for j in range(HALO):
        got = mm_nt(codes, request_hot[REQ * j : REQ * (j + 1), :])
        req_out[j] = jnp.zeros((1, E), F32)
        req_out[j, :, 0:REQ] = got[0:1] + 128.0 * got[1:2] + 2048.0 * (1.0 - got[2:3])

    pl.semaphore_wait(barrier, 7)
    beside = (along(-1, 0), along(1, 0), along(0, -1), along(0, 1), along(0, 0, True))
    requests = [
        pltpu.make_async_remote_copy(
            src_ref=req_out.at[j],
            dst_ref=req_in.at[OPPOSITE[j]],
            send_sem=req_send_sem,
            recv_sem=req_recv_sem,
            device_id=beside[j],
            device_id_type=MESH,
        )
        for j in range(HALO)
    ]
    for copy in requests:
        copy.start()
    greet(round2_sem, nearest)
    ready("psi", "traces", "dense")
    for field in range(5):
        psib[0, 112:128, E * field : E * (field + 1)] = jnp.zeros((16, E), BF16)
        psib[1, 112:128, E * field : E * (field + 1)] = jnp.zeros((16, E), BF16)
        high, low = split(psi[field])
        psib[0, 0:125, E * field : E * (field + 1)] = high
        psib[1, 0:125, E * field : E * (field + 1)] = low
    for half in range(2):
        got = mm(traces_ref[...], psib[half]).astype(BF16)
        for field in range(5):
            for f in range(6):
                xp[160 * half + 32 * field : 160 * half + 32 * (field + 1), E * f : E * (f + 1)] = got[
                    32 * f : 32 * (f + 1), E * field : E * (field + 1)
                ]
        xd[128 * half : 128 * (half + 1), :] = mm(
            dense_ref[...], xp[160 * half : 160 * (half + 1), :]
        ).astype(BF16)

    slots8 = iota((8, E), 0)
    mine = jnp.full((8, E), -1, I32)
    for f in range(6):
        code = jnp.where(offset[f : f + 1] == 0, elem[f : f + 1] + E * nf[f : f + 1], -1)
        mine = jnp.where(slots8 == f, code, mine)
    ready("fo")
    fo = fo_ref[...]
    turned = jnp.concatenate(
        [mine.astype(F32), fo.astype(F32), jnp.zeros((E - 14, E), F32)], 0
    ).T
    columns = iota((E, 6 * E), 1).astype(F32)
    for f in range(6):
        local_hot[E * f : E * (f + 1), :] = one_if(turned[:, f : f + 1] == columns).astype(BF16)
    ready("sweeps", "pen", "penalties", "dt")
    swept[...] = (
        mm(sweeps_ref[0:512], psib[0]) + mm(sweeps_ref[512:1024], psib[0]) + mm(sweeps_ref[0:512], psib[1])
    )
    pen8 = jnp.concatenate([pen_ref[...], jnp.zeros((2, E), F32)], 0)
    pen_terms = []
    for _ in range(3):
        pen_high = pen8.astype(BF16).astype(F32)
        pen_terms.append(pen_high)
        pen8 = pen8 - pen_high
    pen_terms.append(jnp.zeros((8, E), F32))
    pen_nodes[...] = dt_ref[...] * mm(penalties_ref[...], jnp.concatenate(pen_terms, 0).astype(BF16))

    whole(req_in, req_recv_sem).wait()
    pl.semaphore_wait(round2_sem, 7)
    greet(round3_sem, (along(0, 2), along(0, -2), along(8, 0)))
    asked = jnp.zeros((8, E), F32)
    for j in range(HALO):
        asked = jnp.where(slots8 == j, req_in[j], asked)
    asked = jnp.concatenate([asked, jnp.zeros((E - 8, E), F32)], 0).T
    columns = iota((REQ, 6 * E), 1).astype(F32)
    hot = [one_if(asked[0:REQ, j : j + 1] == columns).astype(BF16) for j in range(HALO)]
    answers = mm_nt(jnp.concatenate(hot, 0), xd[...])
    for j in range(HALO):
        resp_out[j] = answers[REQ * j : REQ * (j + 1), :E] + answers[REQ * j : REQ * (j + 1), E:]
    for j in range(HALO):
        pltpu.make_async_remote_copy(
            src_ref=resp_out.at[j],
            dst_ref=resp_in.at[OPPOSITE[j]],
            send_sem=resp_send_sem,
            recv_sem=resp_recv_sem,
            device_id=beside[j],
            device_id_type=MESH,
        ).start()

    @pl.when(s >= 0)
    def _():
        own_answers = mm_nt(local_hot[...], xd[...]).astype(BF16)
        for f in range(6):
            seen = jnp.broadcast_to(turned[:, 8 + f : 9 + f], (E, E))
            for o in range(4):
                mask = one_if(seen == o).astype(BF16)
                for half in range(2):
                    local_turned[E * f : E * (f + 1), 512 * half + E * o : 512 * half + E * (o + 1)] = (
                        own_answers[E * f : E * (f + 1), E * half : E * (half + 1)] * mask
                    )
        ready("turns")
        turns2 = jnp.concatenate([turns_ref[...], turns_ref[...]], 1)
        near[...] = mm_nt(turns2, local_turned[...])
        views = jnp.concatenate(
            [jnp.broadcast_to(fo[f : f + 1], (16, E)).astype(F32).astype(BF16) for f in range(6)], 1
        )
        views = mm_nt(request_hot[...], jnp.concatenate([views] * 8, 0))
        for o in range(4):
            far_masks[o] = one_if(views == o).astype(BF16)

    ready("we", "wf", "wp", "os", "od")
    owner = od_ref[...]
    wall_code = we_ref[...] + E * wf_ref[...]
    for g in range(6):
        wall_hot[E * g : E * (g + 1), :] = one_if(wall_code == iota((E, E), 0) + E * g).astype(BF16)
    for x in range(3):
        for field in range(5):
            wpad[x, field] = jnp.zeros((32, E), F32)
            wpad[x, field, 0:25] = wp[x, 25 * field : 25 * (field + 1)]
    owner_rows = jnp.broadcast_to(owner.astype(F32), (E, E))
    earlier = one_if((owner_rows == owner_rows.T) & (iota((E, E), 0) < iota((E, E), 1)))
    rank = jnp.sum(earlier, axis=0, keepdims=True)
    to_owner[...] = one_if(owner == iota((2 * E, E), 0)).astype(BF16)

    pl.semaphore_wait(round3_sem, 3)
    greet(
        round4_sem,
        (along(1, 2, True), along(-1, -2, True), along(8, 1), along(8, -1), along(6, 0), along(-6, 0)),
    )
    ready("u", "obj", "metric", "visc")
    metric, dt, visc = metric_ref[...], dt_ref[...], visc_ref[...]
    dt_metric, dt_visc = dt * metric, dt * visc

    def lanes(field):
        return slice(E * field, E * (field + 1))

    def transposed_flux(axes, vel, kinetic, enthalpy, weights):
        out = [0.0] * 5
        a_sum = 0.0
        for axis in axes:
            wd, vd = weights[axis], vel[axis]
            carried = wd[1] * vel[0] + wd[2] * vel[1] + wd[3] * vel[2] + enthalpy * wd[4]
            a_sum = a_sum + (wd[1 + axis] + vd * wd[4])
            out[0] = out[0] - vd * carried
            for i in range(3):
                out[1 + i] = out[1 + i] + vd * wd[1 + i]
            out[1 + axis] = out[1 + axis] + (wd[0] + carried)
            out[4] = out[4] + vd * wd[4]
        ga = G * a_sum
        out[0] = out[0] + kinetic * ga
        for i in range(3):
            out[1 + i] = out[1 + i] - vel[i] * ga
        out[4] = out[4] + ga
        return out

    for start in range(0, 125, 8):
        stop = min(start + 8, 125)
        cut = slice(start, stop)
        rho, m1, m2, m3, energy = (u[field, cut] for field in range(5))
        inverse = 1.0 / rho
        vel = (m1 * inverse, m2 * inverse, m3 * inverse)
        kinetic = 0.5 * (vel[0] * vel[0] + vel[1] * vel[1] + vel[2] * vel[2])
        pressure = G * (energy - rho * kinetic)
        enthalpy = (energy + pressure) * inverse
        for i, kept in enumerate((*vel, kinetic, enthalpy)):
            state[i, cut] = kept
        weights = [
            [swept[128 * axis + start : 128 * axis + stop, lanes(field)] for field in range(5)]
            for axis in range(3)
        ]
        out = transposed_flux(range(3), vel, kinetic, enthalpy, weights)
        pen = 1.0 - pen_nodes[384 + start : 384 + stop]
        for field in range(5):
            adj[field, cut] = (
                pen * psi[field, cut]
                + dt * obj[field, cut]
                - dt_metric * out[field]
                - dt_visc * swept[384 + start : 384 + stop, lanes(field)]
            )
    for field in range(5):
        adj[field, 125:128] = jnp.zeros((3, E), F32)
    ready("to_nodes")

    whole(resp_in, resp_recv_sem).wait()
    answered = jnp.concatenate([resp_in[j] for j in range(HALO)], 0)
    answered = split(answered)
    masked = jnp.concatenate(
        [jnp.concatenate([part * far_masks[o] for o in range(4)], 1) for part in answered], 0
    )
    placed = mm_nt(turns_ref[...], masked).astype(BF16)
    far = mm(placed, jnp.concatenate([request_hot[...]] * 2, 0))
    trace = split(near[...] + far)
    jumps = []
    for axis in range(3):
        rhs = jnp.concatenate(
            [
                jnp.concatenate(
                    [
                        trace[half][32 * field : 32 * (field + 1), E * f : E * (f + 1)]
                        for half in range(2)
                        for f in (2 * axis, 2 * axis + 1)
                    ],
                    0,
                )
                for field in range(5)
            ],
            1,
        )
        jumps.append(mm(to_nodes_ref[axis], rhs))

    for start in range(0, 125, 8):
        stop = min(start + 8, 125)
        cut = slice(start, stop)
        axes = range(3) if start < 25 or stop > 100 else range(1, 3)
        vel = tuple(state[i, cut] for i in range(3))
        weights = [[jumps[axis][cut, lanes(field)] for field in range(5)] for axis in range(3)]
        out = transposed_flux(axes, vel, state[3, cut], state[4, cut], weights)
        for field in range(5):
            new = adj[field, cut] - dt_metric * out[field]
            for axis in axes:
                new = new + pen_nodes[128 * axis + start : 128 * axis + stop] * weights[axis][field]
            adj[field, cut] = new
            adj_out[field, cut] = new

    for field in range(5):
        high, low = split(adj[field])
        psib[0, :, E * field : E * (field + 1)] = high
        psib[1, :, E * field : E * (field + 1)] = low
    for half in range(2):
        got = mm(traces_ref[...], psib[half]).astype(BF16)
        for field in range(5):
            for f in range(6):
                xp[160 * half + 32 * field : 160 * half + 32 * (field + 1), E * f : E * (f + 1)] = got[
                    32 * f : 32 * (f + 1), E * field : E * (field + 1)
                ]
    taken = mm(xp[...], wall_hot[...])
    taken = taken[:160] + taken[160:]
    values = [os_ref[...].astype(F32)]
    for x in range(3):
        total = wpad[x, 0] * taken[0:32]
        for field in range(1, 5):
            total = total + wpad[x, field] * taken[32 * field : 32 * (field + 1)]
        values.append(jnp.sum(total, axis=0, keepdims=True))
    mine = jnp.concatenate(values + values, 0)
    mine = jnp.where(rank == lax.shift_right_arithmetic(slots8, 2).astype(F32), mine, 0.0)
    nothing = jnp.zeros((E - 16, E), BF16)
    terms = []
    for _ in range(3):
        term = mine.astype(BF16).astype(F32)
        terms.append(jnp.concatenate([jnp.concatenate([term, jnp.zeros((8, E), F32)], 0).astype(BF16), nothing], 0))
        mine = mine - term
    sent = mm_nt(jnp.concatenate([to_owner[...]] * 3, 1), jnp.concatenate(terms, 1))
    devices = n_span * n_chord * n_wall
    for k in range(devices):
        send_all[k] = sent[k : k + 1]
    pl.semaphore_wait(round4_sem, 6)
    wide = n_span // max(n_span // 4, 1)
    for k, (dy, dx, dz, dw) in enumerate(far_first(n_span, n_chord, n_wall)):
        x = jnp.bitwise_and(s + dx, wide - 1)
        y = jnp.bitwise_and(s + wide * dy, n_span - wide)
        z = jnp.bitwise_and(c + dz, n_chord - 1)
        core = 1 - w if dw else w
        pltpu.make_async_remote_copy(
            src_ref=send_all.at[((y + x) * n_chord + z) * n_wall + core],
            dst_ref=entries_ref.at[k + 1],
            send_sem=all_send_sem,
            recv_sem=all_recv_sem,
            device_id=(y + x, z, core),
            device_id_type=MESH,
        ).start()
    entries_ref[0] = send_all[part]
    whole(req_out, req_send_sem).wait()
    whole(resp_out, resp_send_sem).wait()
    whole(entries_ref.at[1:devices], all_recv_sem).wait()
    whole(send_all.at[1:devices], all_send_sem).wait()


def finish(adj_from, entries_ref, adj_to, sens_to, sens, sems):
    copies = [
        pltpu.make_async_copy(adj_from.at[field], adj_to.at[field], sems.at[field]) for field in range(5)
    ]
    for copy in copies:
        copy.start()
    entries = entries_ref[...].reshape(entries_ref.shape[0], E)
    if entries.shape[0] < 2 * E:
        entries = jnp.concatenate([entries, jnp.zeros((2 * E - entries.shape[0], E), F32)], 0)
    entries = [entries[E * g : E * (g + 1)].T for g in range(2)]
    design = iota((E, E), 0).astype(F32)
    both = jnp.concatenate([e[0:8] for e in entries], 1)
    terms = []
    for _ in range(3):
        term = both.astype(BF16).astype(F32)
        terms.append(term)
        both = both - term
    terms = jnp.concatenate(terms, 0).astype(BF16)
    total = jnp.zeros((3, E), F32)
    for r in range(2):
        hot = jnp.concatenate(
            [one_if(e[4 * r : 4 * r + 1] == design).astype(BF16) for e in entries], 1
        )
        got = mm_nt(terms, hot)
        got = got[0:8] + got[8:16] + got[16:24]
        total = total + got[4 * r + 1 : 4 * r + 4]
    sens[...] = total
    copies.append(pltpu.make_async_copy(sens, sens_to, sems.at[5]))
    copies[5].start()
    for copy in copies:
        copy.wait()


def on_device(sizes, *args):
    (psi, obj, u, metric, dt, visc, pen, fn, nf, fo, we, wf, wp, od, os_) = args
    row = lambda x: x.reshape(1, E)
    vmem = pl.BlockSpec(memory_space=pltpu.VMEM)
    hbm = pl.BlockSpec(memory_space=pltpu.HBM)
    n_span, n_chord, n_wall = sizes
    n_devices = n_span * n_chord * n_wall
    consts = tuple(jnp.asarray(t) for t in tables())
    results = pl.pallas_call(
        functools.partial(kernel, sizes),
        out_shape=(pltpu.VMEM((5, 125, E), F32), pltpu.VMEM((n_devices, 1, E), F32)),
        in_specs=[hbm] * (15 + len(consts)),
        out_specs=(vmem, vmem),
        scratch_shapes=[
            *[pltpu.VMEM((1, E), F32)] * 3,
            pltpu.VMEM((6, E), F32),
            *[pltpu.VMEM((6, E), I32)] * 3,
            *[pltpu.VMEM((1, E), I32)] * 4,
            *[pltpu.VMEM(t.shape, BF16) for t in consts],
            pltpu.VMEM((5, 125, E), F32),
            pltpu.VMEM((5, 125, E), F32),
            pltpu.VMEM((5, 125, E), F32),
            pltpu.VMEM((3, 125, E), F32),
            pltpu.VMEM((3, 5, 32, E), F32),
            pltpu.VMEM((5, 128, E), F32),
            pltpu.VMEM((2, 128, 5 * E), BF16),
            pltpu.VMEM((320, 6 * E), BF16),
            pltpu.VMEM((256, 6 * E), BF16),
            pltpu.VMEM((6 * E, 6 * E), BF16),
            pltpu.VMEM((HALO * REQ, 6 * E), BF16),
            pltpu.VMEM((HALO, 1, E), F32),
            pltpu.VMEM((HALO, 1, E), F32),
            pltpu.VMEM((HALO, REQ, E), F32),
            pltpu.VMEM((HALO, REQ, E), F32),
            pltpu.VMEM((512, 5 * E), F32),
            pltpu.VMEM((512, E), F32),
            pltpu.VMEM((6 * E, 1024), BF16),
            pltpu.VMEM((160, 6 * E), F32),
            pltpu.VMEM((4, HALO * REQ, E), BF16),
            pltpu.VMEM((5, 128, E), F32),
            pltpu.VMEM((3, 128, 5 * E), F32),
            pltpu.VMEM((6 * E, E), BF16),
            pltpu.VMEM((2 * E, E), BF16),
            pltpu.VMEM((n_devices, 1, E), F32),
            pltpu.SemaphoreType.DMA((15 + len(consts),)),
            *[pltpu.SemaphoreType.DMA] * 6,
            *[pltpu.SemaphoreType.REGULAR] * 3,
        ],
        compiler_params=pltpu.CompilerParams(
            collective_id=0, has_side_effects=True, vmem_limit_bytes=58 * 2**20
        ),
        name="adjoint_step",
    )(
        psi,
        obj,
        u,
        wp,
        row(metric),
        row(dt),
        row(visc),
        pen,
        fn,
        nf,
        fo,
        row(we),
        row(wf),
        row(od),
        row(os_),
        *consts,
    )
    return pl.pallas_call(
        finish,
        out_shape=(jax.ShapeDtypeStruct((5, 125, E), F32), jax.ShapeDtypeStruct((3, E), F32)),
        in_specs=[vmem] * 2,
        out_specs=(hbm, hbm),
        scratch_shapes=[pltpu.VMEM((3, E), F32), pltpu.SemaphoreType.DMA((6,))],
        compiler_params=pltpu.CompilerParams(vmem_limit_bytes=16 * 2**20),
        name="results",
    )(*results)


def solution(mesh):
    whole = P(None, None, AXES)
    plane = P(None, AXES)
    line = P(AXES)
    in_specs = (
        (whole,) * 3 + (line,) * 3 + (plane,) * 4 + (line,) * 2 + (whole, P(AXES, None), line)
    )
    sizes = tuple(mesh.shape[name] for name in AXES)
    return jax.shard_map(
        functools.partial(on_device, sizes),
        mesh=mesh,
        in_specs=in_specs,
        out_specs=(whole, plane),
        check_vma=False,
    )
```
